256 devices in a mesh: seq: 8 (over x, core), dp: 32 (over y, z).
Axes of the slice: x: 4, y: 4, z: 8, core: 2. Of those that a mesh axis runs over, the one named last changes fastest.
Arguments:
- inputs: float32 [1024, 65536], P('dp', 'seq'), may hold values from -6 to 6
- cotangent: float32 [1024, 65536], P('dp', 'seq'), may hold values from -6 to 6
- first_factor: float32 [256, 256], replicated, may hold values from -0.375 to 0.375
- second_sequence_factor: float32 [256, 256], replicated, may hold values from -0.375 to 0.375
- inverse_second_factor: float32 [256, 256], replicated, may hold values from -0.375 to 0.375
- inverse_first: float32 [256, 256], replicated, may hold values from -0.375 to 0.375
- twiddle: float32 [256, 256], replicated, may hold values from -4 to 4
- kernel: float32 [1024, 256, 256], P(('dp', 'seq')), may hold values from -5 to 5
- gate_inner: float32 [32, 32, 32], P('dp'), may hold values from -1 to 1
- gate_outer: float32 [32, 32, 32], P('dp'), may hold values from -1 to 1
Outputs:
- layer_out: float32 [1024, 65536], P('dp', 'seq')
- input_grad: float32 [1024, 65536], P('dp', 'seq')
- first_grad: float32 [256, 256], replicated
- second_grad: float32 [256, 256], replicated
- inverse_second_grad: float32 [256, 256], replicated
- inverse_first_grad: float32 [256, 256], replicated
- twiddle_grad: float32 [256, 256], replicated
- kernel_grad: float32 [1024, 256, 256], P(('dp', 'seq'))
- inner_grad: float32 [32, 32, 32], P('dp')
- outer_grad: float32 [32, 32, 32], P('dp')
The draws below stay inside these ranges and needn't reach their ends.
All inputs are finite; a program needn't handle non-finite values.
Results may differ from the reference program's by a relative error of at most 0.00009.
Values sent between devices are 32-bit elements; how exact they have to be, the bound alone decides.
No kernel may reach another device: no remote copies, remote signals or barrier semaphores. Data moves between devices by JAX's collectives and lax.ppermute only.
A program may use at most 128 MiB of HBM per device.

```python
import jax
import jax.numpy as jnp
from jax import lax

C = 1024
CB = 32
PB = 256
NB = 256
LEN = 65536
NCB = 32


def steps_of(key, extent, shards, low, top_value):
    def one(position, shards_of):
        draws = jax.random.uniform(jax.random.fold_in(jax.random.fold_in(key, 6), position), (shards_of,), jnp.float32, low / len(shards), top_value / len(shards))
        return jnp.repeat(jnp.exp(draws), extent[position] // shards_of).reshape((-1,) + (1,) * (len(extent) - position - 1))

    gain = one(*shards[0])
    for cut in shards[1:]:
        gain = gain * one(*cut)
    return gain


def gaussian(own_key, shape, spread, most, shards=(), dtype=jnp.bfloat16):
    values = spread * jax.random.normal(own_key, shape, jnp.float32)
    if shards:
        values = values * steps_of(own_key, shape, shards, -0.22, 0.18)
    return jnp.clip(values, -most, most).astype(dtype)


def setup_inputs(seed: int = 0) -> dict:
    arg_keys = jax.random.split(jax.random.key(seed), 11)
    inputs = gaussian(arg_keys[0], (C, LEN), 1.0, 6.0, ((0, 32), (1, 8)), jnp.float32)
    cotangent = gaussian(arg_keys[1], (C, LEN), 1.0, 6.0, ((0, 32), (1, 8)), jnp.float32)
    first_factor = gaussian(arg_keys[2], (PB, PB), PB ** -0.5, 0.375, (), jnp.float32)
    second_sequence_factor = gaussian(arg_keys[3], (NB, NB), NB ** -0.5, 0.375, (), jnp.float32)
    inverse_second_factor = gaussian(arg_keys[4], (NB, NB), NB ** -0.5, 0.375, (), jnp.float32)
    inverse_first = gaussian(arg_keys[5], (PB, PB), PB ** -0.5, 0.375, (), jnp.float32)
    twiddle = gaussian(arg_keys[6], (NB, PB), 1.0, 4.0, (), jnp.float32)
    kernel = gaussian(arg_keys[7], (C, PB, NB), 1.0, 5.0, ((0, 256),), jnp.float32)
    gate_inner = gaussian(arg_keys[8], (NCB, CB, CB), CB ** -0.5, 1.0, ((0, 32),), jnp.float32)
    gate_outer = gaussian(arg_keys[9], (CB, NCB, NCB), NCB ** -0.5, 1.0, ((0, 32),), jnp.float32)
    return {"inputs": inputs, "cotangent": cotangent, "first_factor": first_factor, "second_sequence_factor": second_sequence_factor, "inverse_second_factor": inverse_second_factor, "inverse_first": inverse_first, "twiddle": twiddle, "kernel": kernel, "gate_inner": gate_inner, "gate_outer": gate_outer}


def contract_product(form, left, right):
    return jnp.einsum(form, left, right, precision=lax.Precision.HIGHEST)

def layer(sequence, first_factor, second_sequence_factor, inverse_second_factor, inverse_first, twiddle, kernel, gate_inner, gate_outer):
    blocked = sequence.reshape(C, NB, PB)
    pre = contract_product('pq,cbq->cbp', first_factor, blocked)
    sectioned_blocks = twiddle * pre
    frequency_spectrum = contract_product('dj,zjx->zxd', second_sequence_factor, sectioned_blocks)
    kernel_scaled = kernel * frequency_spectrum
    unmixed_values = contract_product('bf,kef->kbe', inverse_second_factor, kernel_scaled)
    seq_mixed = contract_product('pq,cbq->cbp', inverse_first, unmixed_values).reshape(C, LEN)
    grouped = sequence.reshape(NCB, CB, LEN)
    within = contract_product('gmk,gkn->gmn', gate_inner, grouped)
    across = contract_product('mhg,gmn->hmn', gate_outer, within).reshape(C, LEN)
    return sequence + seq_mixed * jax.nn.sigmoid(across)

def reference(inputs, cotangent, first_factor, second_sequence_factor, inverse_second_factor, inverse_first, twiddle, kernel, gate_inner, gate_outer):
    output, pullback = jax.vjp(layer, inputs, first_factor, second_sequence_factor, inverse_second_factor, inverse_first, twiddle, kernel, gate_inner, gate_outer)
    grads = pullback(cotangent)
    return (output, grads[0], grads[1], grads[2], grads[3], grads[4], grads[5], grads[6], grads[7], grads[8])
```

```python
import functools

import jax
import jax.numpy as jnp
from jax import lax
from jax.experimental import pallas as pl
from jax.experimental.pallas import tpu as pltpu
from jax.sharding import PartitionSpec as P

F32 = jnp.float32
BF16 = jnp.bfloat16
MIB = 1024 * 1024

NN = (((1,), (0,)), ((), ()))
NT = (((1,), (1,)), ((), ()))
TN = (((0,), (0,)), ((), ()))

SEQ = 8
XS = 4
YS = 4
ZS = 8


def sds(*shape):
    return jax.ShapeDtypeStruct(shape, F32)


VMEM = pl.BlockSpec(memory_space=pltpu.VMEM)
SMEM = pl.BlockSpec(memory_space=pltpu.SMEM)
HBM = pl.BlockSpec(memory_space=pltpu.HBM)
ANY = pl.BlockSpec(memory_space=pl.ANY)

ROWS = (32, 64, 128)
CHUNK = (4, 64, 128)
WIDE = (32, 8192)
CHAN = (1024, 256)
FULL = int(63.7 * MIB)
PARTS = 4
PAIRS = 64 // PARTS // 2


def wide_cut(p):
    return (slice(None), pl.ds(p * 2048, 2048))


def rows_cut(p):
    return (slice(None), pl.ds(p * 16, 16)) if p < PARTS else None


def whole_cut(p):
    return (slice(None),) if p == 0 else None


class Flow:
    def __init__(self):
        self.coming, self.leaving, self.sent = {}, {}, []

    def need(self, k):
        for c in self.coming.pop(k, []):
            c.wait()

    def flush(self, k):
        for c in self.leaving.pop(k, []):
            c.start()
            self.sent.append(c)


def staged(
    body, outs, args, gathers=(), spreads=0, parts=PARTS, index=None, after=(), scratch=(),
    flops=0, limit=FULL, name=None,
):
    n_in, n_out, n_after = len(args), len(outs), len(after)
    flat = [c for g in gathers for c in g]
    chunk_outs = [sds(*CHUNK)] * (SEQ * spreads)
    cut_in = [k for k in range(n_in) if args[k][1] is not None]
    cut_out = [k for k in range(n_out) if outs[k][1] is not None]

    def kernel(*refs):
        refs = list(refs)

        def take(n):
            taken = refs[:n]
            del refs[:n]
            return taken

        place = take(1)[0] if index is not None else None
        in_refs, chunk_refs, _ = take(n_in), take(len(flat)), take(n_after)
        out_refs, spread_refs = take(n_out), take(len(chunk_outs))
        in_bufs, gathered = take(len(cut_in)), take(len(gathers))
        out_bufs, spread = take(len(cut_out)), take(spreads)
        sems = take(1)[0]
        count = [0]

        def copy(source, target):
            made = pltpu.make_async_copy(source, target, sems.at[count[0]])
            count[0] += 1
            return made

        flow = Flow()
        ins, results = list(in_refs), list(out_refs)

        def gather(g):
            arriving = []
            for i in range(SEQ):
                at = pl.ds(lax.rem(place[0] + SEQ - i, SEQ) * 4, 4)
                arriving.append(copy(chunk_refs[g * SEQ + i], gathered[g].at[at]))
                arriving[-1].start()
            flow.coming["rows", g] = arriving

        if gathers:
            gather(0)
        for b, k in enumerate(cut_in):
            ins[k] = in_bufs[b]
        for p in range(parts):
            for b, k in enumerate(cut_in):
                at = args[k][1](p)
                if at is not None:
                    made = copy(in_refs[k].at[at], in_bufs[b].at[at])
                    made.start()
                    flow.coming.setdefault(k if parts == 1 else (k, p), []).append(made)
        for g in range(1, len(gathers)):
            gather(g)
        for b, k in enumerate(cut_out):
            results[k] = out_bufs[b]
            for p in range(parts):
                at = outs[k][1](p)
                if at is not None:
                    flow.leaving.setdefault(k if parts == 1 else (k, p), []).append(
                        copy(out_bufs[b].at[at], out_refs[k].at[at])
                    )
        for s in range(spreads):
            flow.leaving["rows", s] = [
                copy(spread[s].at[pl.ds(lax.rem(place[0] + i, SEQ) * 4, 4)], spread_refs[s * SEQ + i])
                for i in range(SEQ)
            ]
        for p in range(parts):
            if parts > 1:
                for g in range(len(gathers)):
                    flow.need(("rows", g))
                for k in cut_in:
                    flow.need((k, p))
            body(p, flow, ins, gathered, results, spread, refs + [place])
            if parts > 1:
                for k in cut_out:
                    flow.flush((k, p))
        for k in list(flow.coming):
            flow.need(k)
        for k in list(flow.leaving):
            flow.flush(k)
        for c in flow.sent:
            c.wait()

    operands = [a for a, _ in args] + flat + list(after)
    specs = [VMEM if cut is None else ANY for _, cut in args] + [ANY] * (len(flat) + n_after)
    if index is not None:
        operands, specs = [index] + operands, [SMEM] + specs
    n_sems = len(cut_in) * parts + len(flat) + len(cut_out) * parts + len(chunk_outs)
    moved = sum(4 * a.size for a, _ in args) + sum(4 * o.size for o, _ in outs)
    moved += sum(4 * c.size for c in flat) + sum(4 * c.size for c in chunk_outs)
    buffers = [pltpu.VMEM(args[k][0].shape, F32) for k in cut_in]
    buffers += [pltpu.VMEM(ROWS, F32)] * len(gathers)
    buffers += [pltpu.VMEM(outs[k][0].shape, F32) for k in cut_out]
    buffers += [pltpu.VMEM(ROWS, F32)] * spreads
    result = list(
        pl.pallas_call(
            kernel,
            out_shape=[o for o, _ in outs] + chunk_outs,
            in_specs=specs,
            out_specs=[VMEM if cut is None else ANY for _, cut in outs] + [ANY] * len(chunk_outs),
            scratch_shapes=buffers + [pltpu.SemaphoreType.DMA((max(n_sems, 1),))] + list(scratch),
            compiler_params=pltpu.CompilerParams(vmem_limit_bytes=limit),
            cost_estimate=pl.CostEstimate(flops=flops, bytes_accessed=moved, transcendentals=0),
            name=name,
        )(*operands)
    )
    return result[:n_out] + [result[n_out + SEQ * s : n_out + SEQ * (s + 1)] for s in range(spreads)]


def small_call(body, outs, args, scratch=(), index=None, after=(), name=None):
    operands, specs, lead = list(args), [VMEM] * len(args), len(args)
    if index is not None:
        operands, specs, lead = [index] + operands, [SMEM] + specs, lead + 1

    def kernel(*refs):
        body(*refs[:lead], *refs[lead + len(after) :])

    return list(
        pl.pallas_call(
            kernel,
            out_shape=[sds(*o) for o in outs],
            in_specs=specs + [ANY] * len(after),
            out_specs=[VMEM] * len(outs),
            scratch_shapes=list(scratch),
            compiler_params=pltpu.CompilerParams(vmem_limit_bytes=FULL if after else 8 * MIB),
            name=name,
        )(*operands, *after)
    )


def split(value):
    high = value.astype(BF16)
    return high, (value - high.astype(F32)).astype(BF16)


def dot3(left, right, form):
    (lh, ll), (rh, rl) = left, right
    dot = functools.partial(lax.dot_general, dimension_numbers=form, preferred_element_type=F32)
    return dot(lh, rh) + (dot(lh, rl) + dot(ll, rh))


def aligned(offset, step):
    return pl.multiple_of(offset, step)


def pairs_of(p):
    return range(p * PAIRS, (p + 1) * PAIRS)


def columns(j):
    return slice(j * 256, (j + 1) * 256)


def get_rows(ref, j):
    return jnp.concatenate([ref[:, 2 * j, :], ref[:, 2 * j + 1, :]], axis=1)


def put_rows(ref, j, value):
    ref[:, 2 * j, :] = value[:, :128]
    ref[:, 2 * j + 1, :] = value[:, 128:]


def within_body(p, flow, ins, gathered, outs, spread, scratch):
    x, inner = ins
    weight = split(inner[...])
    for j in pairs_of(p):
        put_rows(outs[0], j, dot3(weight, split(x[:, columns(j)]), NN))


def x_rows_body(p, flow, ins, gathered, outs, spread, scratch):
    for j in pairs_of(p):
        put_rows(spread[0], j, ins[0][:, columns(j)])


def gate_body(p, flow, ins, gathered, outs, spread, scratch):
    within, outer = ins
    weight = split(outer[...])
    for j in pairs_of(p):
        put_rows(outs[0], j, jax.nn.sigmoid(dot3(weight, split(get_rows(within, j)), NN)))


def weigh_body(p, flow, ins, gathered, outs, spread, scratch):
    for j in pairs_of(p):
        put_rows(outs[0], j, ins[0][:, columns(j)] * get_rows(gathered[0], j))


def across_grad_body(p, flow, ins, gathered, outs, spread, scratch):
    weighed, gate = ins
    at = (slice(None), slice(p * 16, (p + 1) * 16))
    g = gate[at]
    outs[0][at] = weighed[at] * g * (1.0 - g)


def mixed_grad_body(p, flow, ins, gathered, outs, spread, scratch):
    for j in pairs_of(p):
        put_rows(spread[0], j, ins[0][:, columns(j)] * get_rows(ins[1], j))


def output_body(p, flow, ins, gathered, outs, spread, scratch):
    x, gate = ins
    for j in pairs_of(p):
        outs[0][:, columns(j)] = x[:, columns(j)] + get_rows(gathered[0], j) * get_rows(gate, j)


def within_grad_body(p, flow, ins, gathered, outs, spread, scratch):
    across_grad, outer = ins
    weight = split(outer[...].T)
    for j in pairs_of(p):
        put_rows(outs[0], j, dot3(weight, split(get_rows(across_grad, j)), NN))


def outer_grad_body(p, flow, ins, gathered, outs, spread, scratch):
    total = outs[0][...] if p else jnp.zeros((32, 32), F32)
    for j in pairs_of(p):
        total = total + dot3(split(get_rows(ins[0], j)), split(get_rows(ins[1], j)), NT)
    outs[0][...] = total


def inner_grad_body(p, flow, ins, gathered, outs, spread, scratch):
    within_grad, x, outer_part = ins
    held = scratch[0]
    total = held[...] if p else jnp.zeros((32, 32), F32)
    for j in pairs_of(p):
        total = total + dot3(split(get_rows(within_grad, j)), split(x[:, columns(j)]), NT)
    held[...] = total
    if p == PARTS - 1:
        out = outs[0]
        out[...] = jnp.zeros_like(out)
        for k in range(2):
            rows = slice(16 * k, 16 * k + 16)
            out[:, 128 * k : 128 * k + 32] = held[rows, :]
            out[:, 128 * k + 32 : 128 * k + 64] = outer_part[rows, :]


def input_grad_body(p, flow, ins, gathered, outs, spread, scratch):
    cot, within_grad, inner = ins
    weight = split(inner[...].T)
    for j in pairs_of(p):
        product = dot3(weight, split(get_rows(within_grad, j)), NN)
        outs[0][:, columns(j)] = (cot[:, columns(j)] + get_rows(gathered[0], j)) + product


def assemble(c, chunks, out, start):
    for s in range(SEQ):
        at = slice(start + s * 32, start + (s + 1) * 32)
        out[at, 0:128] = chunks[s * 4 + c, pl.ds(0, 32, stride=2), :]
        out[at, 128:256] = chunks[s * 4 + c, pl.ds(1, 32, stride=2), :]


def disperse(c, value, chunks):
    for s in range(SEQ):
        rows = value[s * 32 : (s + 1) * 32, :]
        chunks[s * 4 + c, pl.ds(0, 32, stride=2), :] = rows[:, :128]
        chunks[s * 4 + c, pl.ds(1, 32, stride=2), :] = rows[:, 128:]


def channel(c):
    return slice(c * 256, (c + 1) * 256)


def forward_body(p, flow, ins, gathered, outs, spread, scratch):
    first, twiddle, second, kernel, inverse_second, inverse_first = ins
    pre, spectrum, unmixed = outs
    x = scratch[0]
    flow.need(("rows", 0))
    flow.need(0)
    weight = split(first[...])
    for c in range(4):
        assemble(c, gathered[0], x, c * 256)
        pre[channel(c), :] = dot3(split(x[channel(c), :]), weight, NT)
    flow.flush(0)
    flow.need(1)
    flow.need(2)
    weight = split(second[...])
    for c in range(4):
        spectrum[channel(c), :] = dot3(weight, split(twiddle[...] * pre[channel(c), :]), NN)
    flow.flush(1)
    flow.need(3)
    flow.need(4)
    weight = split(inverse_second[...])
    for c in range(4):
        unmixed[channel(c), :] = dot3(weight, split(kernel[c].T * spectrum[channel(c), :]), NN)
    flow.flush(2)
    flow.need(5)
    weight = split(inverse_first[...])
    for c in range(4):
        disperse(c, dot3(split(unmixed[channel(c), :]), weight, NT), spread[0])


def add_up(terms):
    total = terms[0]
    for term in terms[1:]:
        total = total + term
    return total


def backward_body(p, flow, ins, gathered, outs, spread, scratch):
    inverse_first, unmixed, inverse_second, kernel, spectrum, second, twiddle, pre, first = ins
    series, kernel_grad, keep, send = outs
    x, mixed_grad, work, unmixed_grad, total, place = scratch
    flow.need(("rows", 0))
    flow.need(0)
    weight = split(inverse_first[...])
    for c in range(4):
        assemble(c, gathered[0], mixed_grad, c * 256)
        unmixed_grad[channel(c), :] = dot3(split(mixed_grad[channel(c), :]), weight, NN)
    flow.need(1)
    total[768:1024, :] = dot3(split(mixed_grad[...]), split(unmixed[...]), TN)
    flow.need(2)
    flow.need(3)
    flow.need(4)
    weight = split(inverse_second[...].T)
    terms = []
    for c in range(4):
        du = split(unmixed_grad[channel(c), :])
        kt = kernel[c].T
        sp = spectrum[channel(c), :]
        dsc = dot3(weight, du, NN)
        kernel_grad[c] = (dsc * sp).T
        work[channel(c), :] = dsc * kt
        terms.append(dot3(du, split(kt * sp), NT))
    total[512:768, :] = add_up(terms)
    flow.flush(1)
    flow.need(5)
    flow.need(6)
    flow.need(7)
    weight = split(second[...].T)
    terms, twiddles = [], []
    for c in range(4):
        dsp = split(work[channel(c), :])
        ds = dot3(weight, dsp, NN)
        product = pre[channel(c), :]
        terms.append(dot3(dsp, split(twiddle[...] * product), NT))
        twiddles.append(ds * product)
        mixed_grad[channel(c), :] = ds * twiddle[...]
    total[256:512, :] = add_up(terms)
    total[1024:1280, :] = add_up(twiddles)
    flow.need(("rows", 1))
    flow.need(8)
    weight = split(first[...])
    for c in range(4):
        assemble(c, gathered[1], x, c * 256)
        series[channel(c), :] = dot3(split(mixed_grad[channel(c), :]), weight, NN)
    total[0:256, :] = dot3(split(mixed_grad[...]), split(x[...]), TN)
    core = lax.rem(place[0], 2)
    keep[...] = total[pl.ds(aligned(core * 640, 640), 640), :]
    send[...] = total[pl.ds(aligned((1 - core) * 640, 640), 640), :]


def series_body(p, flow, ins, gathered, outs, spread, scratch):
    flow.need(0)
    for c in range(4):
        disperse(c, ins[0][channel(c), :], spread[0])


def sum_core_body(index, keep, got, *refs):
    outs, total = refs[:XS], refs[XS]
    total[...] = keep[...] + got[...]
    place = index[0] // 2
    for k in range(XS):
        outs[k][...] = total[pl.ds(aligned(lax.rem(place + k, XS) * 160, 160), 160), :]


def sum_x_body(index, a, b, c, d, *refs):
    outs, total = refs[:YS], refs[YS]
    total[...] = (a[...] + b[...]) + (c[...] + d[...])
    place = index[1] // ZS
    for k in range(YS):
        outs[k][...] = total[pl.ds(aligned(lax.rem(place + k, YS) * 40, 40), 40), :]


def sum_y_body(a, b, c, d, out):
    out[...] = (a[...] + b[...]) + (c[...] + d[...])


def add_body(a, b, out):
    out[...] = a[...] + b[...]


def join_y_body(index, a, b, c, d, gate_part, out):
    place = index[1] // ZS
    for k, part in enumerate((a, b, c, d)):
        origin = lax.rem(place + YS - k, YS)
        out[pl.ds(aligned(origin * 40, 40), 40), :] = part[...]
    out[160:176, :] = gate_part[...]


def join_x_body(index, a, b, c, d, out, slots):
    place = index[0] // 2
    for k, part in enumerate((a, b, c, d)):
        origin = lax.rem(place + XS - k, XS)
        out[pl.ds(aligned(origin * 160, 160), 160), :] = part[0:160, :]
        slots[origin] = part[160:176, :]
    out[640:656, :] = (slots[0] + slots[1]) + (slots[2] + slots[3])


def join_core_body(index, mine, other, *refs):
    outs, (inner, outer, total) = refs[:5], refs[5:]
    core = lax.rem(index[0], 2)
    total[pl.ds(aligned(core * 640, 640), 640), :] = mine[0:640, :]
    total[pl.ds(aligned((1 - core) * 640, 640), 640), :] = other[0:640, :]
    for k in range(5):
        outs[k][...] = total[k * 256 : (k + 1) * 256, :]
    gate = mine[640:656, :] + other[640:656, :]
    for k in range(2):
        rows = slice(16 * k, 16 * k + 16)
        inner[rows, :] = gate[:, 128 * k : 128 * k + 32]
        outer[rows, :] = gate[:, 128 * k + 32 : 128 * k + 64]


def exchange_seq(chunks):
    return [chunks[0]] + [
        lax.ppermute(chunks[i], "seq", [(s, (s + i) % SEQ) for s in range(SEQ)])
        for i in range(1, SEQ)
    ]


def swap_core(value):
    return lax.ppermute(value, "seq", [(s, s ^ 1) for s in range(SEQ)])


def shift_x(value, k):
    return lax.ppermute(value, "seq", [(s, (s + 2 * k) % SEQ) for s in range(SEQ)])


def shift_y(value, k):
    pairs = [(y * ZS + z, (y + k) % YS * ZS + z) for y in range(YS) for z in range(ZS)]
    return lax.ppermute(value, "dp", pairs)


def swap_dp(value, flip):
    return lax.ppermute(value, "dp", [(d, d ^ flip) for d in range(YS * ZS)])


def exchange_dp(value):
    return lax.all_to_all(value, "dp", 0, 0, tiled=True)


def per_device(
    inputs,
    cotangent,
    first_factor,
    second_sequence_factor,
    inverse_second_factor,
    inverse_first,
    twiddle,
    kernel,
    gate_inner,
    gate_outer,
):
    index = jnp.stack([lax.axis_index("seq"), lax.axis_index("dp")]).astype(jnp.int32)
    inner, outer = (gate_inner[0], whole_cut), (gate_outer[0], whole_cut)
    first, second, inverse_second, inverse_1st, twid, spectral = [
        (f, whole_cut)
        for f in (
            first_factor, second_sequence_factor, inverse_second_factor, inverse_first, twiddle, kernel
        )
    ]
    x, cot = (inputs, wide_cut), (cotangent, wide_cut)
    rows_out, wide_out, chan_out = (sds(*ROWS), rows_cut), (sds(*WIDE), wide_cut), (sds(*CHAN), whole_cut)
    vchan = pltpu.VMEM(CHAN, F32)
    small = 2 * 3 * 32 * 32 * 8192
    product = 2 * 3 * 1024 * 256 * 256

    (within,) = staged(within_body, [rows_out], [x, inner], flops=small, name="within")
    within_spread = exchange_dp(within)

    (x_chunks,) = staged(x_rows_body, [], [x], spreads=1, index=index, name="x_rows")
    x_chunks = exchange_seq(x_chunks)
    pre, spectrum, unmixed, mixed_chunks = staged(
        forward_body, [chan_out] * 3, [first, twid, second, spectral, inverse_second, inverse_1st],
        [x_chunks], 1, 1, index, scratch=[vchan], flops=4 * product, name="forward",
    )
    mixed_chunks = exchange_seq(mixed_chunks)

    (gate_spread,) = staged(
        gate_body, [rows_out], [(within_spread, rows_cut), outer], after=[pre], flops=small,
        name="gate",
    )
    gate = exchange_dp(gate_spread)
    (weighed,) = staged(weigh_body, [rows_out], [cot], [mixed_chunks], index=index, name="weigh")
    (across_grad,) = staged(
        across_grad_body, [rows_out], [(weighed, rows_cut), (gate, rows_cut)], name="across_grad"
    )
    across_grad_spread = exchange_dp(across_grad)
    (grad_chunks,) = staged(
        mixed_grad_body, [], [cot, (gate, rows_cut)], spreads=1, index=index, after=[across_grad],
        name="mixed_grad",
    )
    (output,) = staged(
        output_body, [wide_out], [x, (gate, rows_cut)], [mixed_chunks], index=index,
        after=[grad_chunks[0]], name="output",
    )
    grad_chunks = exchange_seq(grad_chunks)

    series, kernel_grad, keep, send = staged(
        backward_body,
        [chan_out, (sds(4, 256, 256), whole_cut), (sds(640, 256), None), (sds(640, 256), None)],
        [
            inverse_1st, (unmixed, whole_cut), inverse_second, spectral, (spectrum, whole_cut), second,
            twid, (pre, whole_cut), first,
        ],
        [grad_chunks, x_chunks], 0, 1, index, [output],
        [vchan, vchan, vchan, vchan, pltpu.VMEM((1280, 256), F32)],
        flops=8 * product, name="backward",
    )
    (within_grad_spread,) = staged(
        within_grad_body, [rows_out], [(across_grad_spread, rows_cut), outer], after=[keep],
        flops=small, name="within_grad",
    )
    within_grad = exchange_dp(within_grad_spread)
    got = swap_core(send)
    quarters = small_call(
        sum_core_body, [(160, 256)] * XS, [keep, got], [pltpu.VMEM((640, 256), F32)], index,
        [within_grad_spread], "sum_core",
    )
    quarters = [quarters[0]] + [shift_x(quarters[k], k) for k in range(1, XS)]
    parts = small_call(
        sum_x_body, [(40, 256)] * YS, quarters, [pltpu.VMEM((160, 256), F32)], index, name="sum_x"
    )

    parts = [parts[0]] + [shift_y(parts[k], k) for k in range(1, YS)]
    (series_chunks,) = staged(
        series_body, [], [(series, whole_cut)], spreads=1, parts=1, index=index, after=[parts[0]],
        name="series_rows",
    )
    (part,) = small_call(
        sum_y_body, [(40, 256)], parts, after=[series_chunks[0]], name="sum_y"
    )
    got = swap_dp(part, 1)
    series_chunks = exchange_seq(series_chunks)
    (part,) = small_call(add_body, [(40, 256)], [part, got], after=series_chunks[1:3], name="sum_z")
    got = swap_dp(part, 2)
    (outer_part,) = staged(
        outer_grad_body, [(sds(32, 32), None)],
        [(across_grad_spread, rows_cut), (within_spread, rows_cut)], after=[part], flops=small,
        name="outer_grad",
    )
    (part,) = small_call(add_body, [(40, 256)], [part, got], after=[outer_part], name="sum_z")
    got = swap_dp(part, 4)
    (part,) = small_call(add_body, [(40, 256)], [part, got], name="sum_z")
    parts = [part] + [shift_y(part, k) for k in range(1, YS)]
    (gate_part,) = staged(
        inner_grad_body, [(sds(16, 256), None)],
        [(within_grad, rows_cut), x, (outer_part, whole_cut)], after=[part],
        scratch=[pltpu.VMEM((32, 32), F32)], flops=small, name="inner_grad",
    )
    (part,) = small_call(
        join_y_body, [(176, 256)], parts + [gate_part], index=index, name="join_y"
    )
    parts = [part] + [shift_x(part, k) for k in range(1, XS)]
    (input_grad,) = staged(
        input_grad_body, [wide_out], [cot, (within_grad, rows_cut), inner], [series_chunks],
        index=index, after=[part], flops=small, name="input_grad",
    )
    (half,) = small_call(
        join_x_body, [(656, 256)], parts, [pltpu.VMEM((XS, 16, 256), F32)], index, name="join_x"
    )
    *totals, inner_total, outer_total = small_call(
        join_core_body, [(256, 256)] * 5 + [(32, 32)] * 2, [half, swap_core(half)],
        [pltpu.VMEM((1280, 256), F32)], index, name="join_core",
    )
    first_total, second_total, inverse_second_total, inverse_first_total, twiddle_total = totals
    return (
        output,
        input_grad,
        first_total,
        second_total,
        inverse_second_total,
        inverse_first_total,
        twiddle_total,
        kernel_grad,
        inner_total[None],
        outer_total[None],
    )


def solution(mesh):
    wide = P("dp", "seq")
    gate = P("dp", None, None)
    spectral = P(("dp", "seq"), None, None)
    return jax.shard_map(
        per_device,
        mesh=mesh,
        in_specs=(wide, wide, P(), P(), P(), P(), P(), spectral, gate, gate),
        out_specs=(wide, wide, P(), P(), P(), P(), P(), spectral, gate, gate),
        check_vma=False,
    )
```

```python
import functools

import jax
import jax.numpy as jnp
from jax import lax
from jax.experimental import pallas as pl
from jax.experimental.pallas import tpu as pltpu
from jax.sharding import PartitionSpec as P

F32 = jnp.float32
BF16 = jnp.bfloat16
MIB = 1024 * 1024

NN = (((1,), (0,)), ((), ()))
NT = (((1,), (1,)), ((), ()))
TN = (((0,), (0,)), ((), ()))

SEQ = 8
XS = 4
YS = 4
ZS = 8


def sds(*shape):
    return jax.ShapeDtypeStruct(shape, F32)


VMEM = pl.BlockSpec(memory_space=pltpu.VMEM)
SMEM = pl.BlockSpec(memory_space=pltpu.SMEM)
HBM = pl.BlockSpec(memory_space=pltpu.HBM)
ANY = pl.BlockSpec(memory_space=pl.ANY)

ROWS = (32, 64, 128)
CHUNK = (4, 64, 128)
WIDE = (32, 8192)
CHAN = (1024, 256)
FULL = int(63.7 * MIB)
NEAR = int(63.2 * MIB)
PARTS = 4
PAIRS = 64 // PARTS // 2


def wide_cut(p):
    return (slice(None), pl.ds(p * 2048, 2048))


def rows_cut(p):
    return (slice(None), pl.ds(p * 16, 16)) if p < PARTS else None


def whole_cut(p):
    return (slice(None),) if p == 0 else None


class Flow:
    def __init__(self):
        self.coming, self.leaving, self.sent = {}, {}, []

    def need(self, k):
        for c in self.coming.pop(k, []):
            c.wait()

    def flush(self, k):
        for c in self.leaving.pop(k, []):
            c.start()
            self.sent.append(c)


def staged(
    body, outs, args, gathers=(), spreads=0, parts=PARTS, index=None, after=(), scratch=(),
    flops=0, limit=FULL, name=None,
):
    n_in, n_out, n_after = len(args), len(outs), len(after)
    flat = [c for g in gathers for c in g]
    chunk_outs = [sds(*CHUNK)] * (SEQ * spreads)
    cut_in = [k for k in range(n_in) if args[k][1] is not None]
    cut_out = [k for k in range(n_out) if outs[k][1] is not None]

    def kernel(*refs):
        refs = list(refs)

        def take(n):
            taken = refs[:n]
            del refs[:n]
            return taken

        place = take(1)[0] if index is not None else None
        in_refs, chunk_refs, _ = take(n_in), take(len(flat)), take(n_after)
        out_refs, spread_refs = take(n_out), take(len(chunk_outs))
        in_bufs, gathered = take(len(cut_in)), take(len(gathers))
        out_bufs, spread = take(len(cut_out)), take(spreads)
        sems = take(1)[0]
        count = [0]

        def copy(source, target):
            made = pltpu.make_async_copy(source, target, sems.at[count[0]])
            count[0] += 1
            return made

        flow = Flow()
        ins, results = list(in_refs), list(out_refs)

        def gather(g):
            arriving = []
            for i in range(SEQ):
                at = pl.ds(lax.rem(place[0] + SEQ - i, SEQ) * 4, 4)
                arriving.append(copy(chunk_refs[g * SEQ + i], gathered[g].at[at]))
                arriving[-1].start()
            flow.coming["rows", g] = arriving

        if gathers:
            gather(0)
        for b, k in enumerate(cut_in):
            ins[k] = in_bufs[b]
        for p in range(parts):
            for b, k in enumerate(cut_in):
                at = args[k][1](p)
                if at is not None:
                    made = copy(in_refs[k].at[at], in_bufs[b].at[at])
                    made.start()
                    flow.coming.setdefault(k if parts == 1 else (k, p), []).append(made)
        for g in range(1, len(gathers)):
            gather(g)
        for b, k in enumerate(cut_out):
            results[k] = out_bufs[b]
            for p in range(parts):
                at = outs[k][1](p)
                if at is not None:
                    flow.leaving.setdefault(k if parts == 1 else (k, p), []).append(
                        copy(out_bufs[b].at[at], out_refs[k].at[at])
                    )
        for s in range(spreads):
            flow.leaving["rows", s] = [
                copy(spread[s].at[pl.ds(lax.rem(place[0] + i, SEQ) * 4, 4)], spread_refs[s * SEQ + i])
                for i in range(SEQ)
            ]
        for p in range(parts):
            if parts > 1:
                for g in range(len(gathers)):
                    flow.need(("rows", g))
                for k in cut_in:
                    flow.need((k, p))
            body(p, flow, ins, gathered, results, spread, refs + [place])
            if parts > 1:
                for k in cut_out:
                    flow.flush((k, p))
        for k in list(flow.coming):
            flow.need(k)
        for k in list(flow.leaving):
            flow.flush(k)
        for c in flow.sent:
            c.wait()

    operands = [a for a, _ in args] + flat + list(after)
    specs = [VMEM if cut is None else ANY for _, cut in args] + [ANY] * (len(flat) + n_after)
    if index is not None:
        operands, specs = [index] + operands, [SMEM] + specs
    n_sems = len(cut_in) * parts + len(flat) + len(cut_out) * parts + len(chunk_outs)
    moved = sum(4 * a.size for a, _ in args) + sum(4 * o.size for o, _ in outs)
    moved += sum(4 * c.size for c in flat) + sum(4 * c.size for c in chunk_outs)
    buffers = [pltpu.VMEM(args[k][0].shape, F32) for k in cut_in]
    buffers += [pltpu.VMEM(ROWS, F32)] * len(gathers)
    buffers += [pltpu.VMEM(outs[k][0].shape, F32) for k in cut_out]
    buffers += [pltpu.VMEM(ROWS, F32)] * spreads
    result = list(
        pl.pallas_call(
            kernel,
            out_shape=[o for o, _ in outs] + chunk_outs,
            in_specs=specs,
            out_specs=[VMEM if cut is None else ANY for _, cut in outs] + [ANY] * len(chunk_outs),
            scratch_shapes=buffers + [pltpu.SemaphoreType.DMA((max(n_sems, 1),))] + list(scratch),
            compiler_params=pltpu.CompilerParams(vmem_limit_bytes=limit),
            cost_estimate=pl.CostEstimate(flops=flops, bytes_accessed=moved, transcendentals=0),
            name=name,
        )(*operands)
    )
    return result[:n_out] + [result[n_out + SEQ * s : n_out + SEQ * (s + 1)] for s in range(spreads)]


def small_call(body, outs, args, scratch=(), index=None, after=(), name=None):
    operands, specs, lead = list(args), [VMEM] * len(args), len(args)
    if index is not None:
        operands, specs, lead = [index] + operands, [SMEM] + specs, lead + 1

    def kernel(*refs):
        body(*refs[:lead], *refs[lead + len(after) :])

    return list(
        pl.pallas_call(
            kernel,
            out_shape=[sds(*o) for o in outs],
            in_specs=specs + [ANY] * len(after),
            out_specs=[VMEM] * len(outs),
            scratch_shapes=list(scratch),
            compiler_params=pltpu.CompilerParams(vmem_limit_bytes=NEAR if after else 8 * MIB),
            name=name,
        )(*operands, *after)
    )


def split(value):
    high = value.astype(BF16)
    return high, (value - high.astype(F32)).astype(BF16)


def dot3(left, right, form):
    (lh, ll), (rh, rl) = left, right
    dot = functools.partial(lax.dot_general, dimension_numbers=form, preferred_element_type=F32)
    return dot(lh, rh) + (dot(lh, rl) + dot(ll, rh))


def aligned(offset, step):
    return pl.multiple_of(offset, step)


def pairs_of(p):
    return range(p * PAIRS, (p + 1) * PAIRS)


def columns(j):
    return slice(j * 256, (j + 1) * 256)


def get_rows(ref, j):
    return jnp.concatenate([ref[:, 2 * j, :], ref[:, 2 * j + 1, :]], axis=1)


def put_rows(ref, j, value):
    ref[:, 2 * j, :] = value[:, :128]
    ref[:, 2 * j + 1, :] = value[:, 128:]


def within_body(p, flow, ins, gathered, outs, spread, scratch):
    x, inner = ins
    weight = split(inner[...])
    for j in pairs_of(p):
        put_rows(outs[0], j, dot3(weight, split(x[:, columns(j)]), NN))


def x_rows_body(p, flow, ins, gathered, outs, spread, scratch):
    for j in pairs_of(p):
        put_rows(spread[0], j, ins[0][:, columns(j)])


def gate_body(p, flow, ins, gathered, outs, spread, scratch):
    within, outer = ins
    weight = split(outer[...])
    for j in pairs_of(p):
        put_rows(outs[0], j, jax.nn.sigmoid(dot3(weight, split(get_rows(within, j)), NN)))


def weigh_body(p, flow, ins, gathered, outs, spread, scratch):
    for j in pairs_of(p):
        put_rows(outs[0], j, ins[0][:, columns(j)] * get_rows(gathered[0], j))


def across_grad_body(p, flow, ins, gathered, outs, spread, scratch):
    weighed, gate = ins
    at = (slice(None), slice(p * 16, (p + 1) * 16))
    g = gate[at]
    outs[0][at] = weighed[at] * g * (1.0 - g)


def mixed_grad_body(p, flow, ins, gathered, outs, spread, scratch):
    for j in pairs_of(p):
        put_rows(spread[0], j, ins[0][:, columns(j)] * get_rows(ins[1], j))


def output_body(p, flow, ins, gathered, outs, spread, scratch):
    x, gate = ins
    for j in pairs_of(p):
        outs[0][:, columns(j)] = x[:, columns(j)] + get_rows(gathered[0], j) * get_rows(gate, j)


def within_grad_body(p, flow, ins, gathered, outs, spread, scratch):
    across_grad, outer = ins
    weight = split(outer[...].T)
    for j in pairs_of(p):
        put_rows(outs[0], j, dot3(weight, split(get_rows(across_grad, j)), NN))


def outer_grad_body(p, flow, ins, gathered, outs, spread, scratch):
    total = outs[0][...] if p else jnp.zeros((32, 32), F32)
    for j in pairs_of(p):
        total = total + dot3(split(get_rows(ins[0], j)), split(get_rows(ins[1], j)), NT)
    outs[0][...] = total


def inner_grad_body(p, flow, ins, gathered, outs, spread, scratch):
    within_grad, x, outer_part = ins
    held = scratch[0]
    total = held[...] if p else jnp.zeros((32, 32), F32)
    for j in pairs_of(p):
        total = total + dot3(split(get_rows(within_grad, j)), split(x[:, columns(j)]), NT)
    held[...] = total
    if p == PARTS - 1:
        out = outs[0]
        out[...] = jnp.zeros_like(out)
        for k in range(2):
            rows = slice(16 * k, 16 * k + 16)
            out[:, 128 * k : 128 * k + 32] = held[rows, :]
            out[:, 128 * k + 32 : 128 * k + 64] = outer_part[rows, :]


def input_grad_body(p, flow, ins, gathered, outs, spread, scratch):
    cot, series, within_grad, inner = ins
    weight = split(inner[...].T)
    for j in pairs_of(p):
        product = dot3(weight, split(get_rows(within_grad, j)), NN)
        outs[0][:, columns(j)] = (cot[:, columns(j)] + get_rows(series, j)) + product


def assemble(c, chunks, out, start):
    for s in range(SEQ):
        at = slice(start + s * 32, start + (s + 1) * 32)
        out[at, 0:128] = chunks[s * 4 + c, pl.ds(0, 32, stride=2), :]
        out[at, 128:256] = chunks[s * 4 + c, pl.ds(1, 32, stride=2), :]


def disperse(c, value, chunks):
    for s in range(SEQ):
        rows = value[s * 32 : (s + 1) * 32, :]
        chunks[s * 4 + c, pl.ds(0, 32, stride=2), :] = rows[:, :128]
        chunks[s * 4 + c, pl.ds(1, 32, stride=2), :] = rows[:, 128:]


def channel(c):
    return slice(c * 256, (c + 1) * 256)


def forward_body(p, flow, ins, gathered, outs, spread, scratch):
    first, twiddle, second, kernel, inverse_second, inverse_first = ins
    pre, spectrum, unmixed = outs
    x = scratch[0]
    flow.need(("rows", 0))
    flow.need(0)
    weight = split(first[...])
    for c in range(4):
        assemble(c, gathered[0], x, c * 256)
        pre[channel(c), :] = dot3(split(x[channel(c), :]), weight, NT)
    flow.flush(0)
    flow.need(1)
    flow.need(2)
    weight = split(second[...])
    for c in range(4):
        spectrum[channel(c), :] = dot3(weight, split(twiddle[...] * pre[channel(c), :]), NN)
    flow.flush(1)
    flow.need(3)
    flow.need(4)
    weight = split(inverse_second[...])
    for c in range(4):
        unmixed[channel(c), :] = dot3(weight, split(kernel[c].T * spectrum[channel(c), :]), NN)
    flow.flush(2)
    flow.need(5)
    weight = split(inverse_first[...])
    for c in range(4):
        disperse(c, dot3(split(unmixed[channel(c), :]), weight, NT), spread[0])


def add_up(terms):
    total = terms[0]
    for term in terms[1:]:
        total = total + term
    return total


def backward_body(p, flow, ins, gathered, outs, spread, scratch):
    inverse_first, unmixed, inverse_second, kernel, spectrum, second, twiddle, pre, first = ins
    series, kernel_grad, keep, send = outs
    x, mixed_grad, work, unmixed_grad, total, place = scratch
    flow.need(("rows", 0))
    flow.need(0)
    weight = split(inverse_first[...])
    for c in range(4):
        assemble(c, gathered[0], mixed_grad, c * 256)
        unmixed_grad[channel(c), :] = dot3(split(mixed_grad[channel(c), :]), weight, NN)
    flow.need(1)
    total[768:1024, :] = dot3(split(mixed_grad[...]), split(unmixed[...]), TN)
    flow.need(2)
    flow.need(3)
    flow.need(4)
    weight = split(inverse_second[...].T)
    terms = []
    for c in range(4):
        du = split(unmixed_grad[channel(c), :])
        kt = kernel[c].T
        sp = spectrum[channel(c), :]
        dsc = dot3(weight, du, NN)
        kernel_grad[c] = (dsc * sp).T
        work[channel(c), :] = dsc * kt
        terms.append(dot3(du, split(kt * sp), NT))
    total[512:768, :] = add_up(terms)
    flow.flush(1)
    flow.need(5)
    flow.need(6)
    flow.need(7)
    weight = split(second[...].T)
    terms, twiddles = [], []
    for c in range(4):
        dsp = split(work[channel(c), :])
        ds = dot3(weight, dsp, NN)
        product = pre[channel(c), :]
        terms.append(dot3(dsp, split(twiddle[...] * product), NT))
        twiddles.append(ds * product)
        mixed_grad[channel(c), :] = ds * twiddle[...]
    total[256:512, :] = add_up(terms)
    total[1024:1280, :] = add_up(twiddles)
    flow.need(("rows", 1))
    flow.need(8)
    weight = split(first[...])
    for c in range(4):
        assemble(c, gathered[1], x, c * 256)
        series[channel(c), :] = dot3(split(mixed_grad[channel(c), :]), weight, NN)
    total[0:256, :] = dot3(split(mixed_grad[...]), split(x[...]), TN)
    flow.flush(0)
    core = lax.rem(place[0], 2)
    keep[...] = total[pl.ds(aligned(core * 640, 640), 640), :]
    send[...] = total[pl.ds(aligned((1 - core) * 640, 640), 640), :]


def series_body(p, flow, ins, gathered, outs, spread, scratch):
    flow.need(0)
    for c in range(4):
        disperse(c, ins[0][channel(c), :], outs[0])


def sum_core_body(index, keep, got, *refs):
    outs, total = refs[:XS], refs[XS]
    total[...] = keep[...] + got[...]
    place = index[0] // 2
    for k in range(XS):
        outs[k][...] = total[pl.ds(aligned(lax.rem(place + k, XS) * 160, 160), 160), :]


def sum_x_body(index, a, b, c, d, *refs):
    outs, total = refs[:YS], refs[YS]
    total[...] = (a[...] + b[...]) + (c[...] + d[...])
    place = index[1] // ZS
    for k in range(YS):
        outs[k][...] = total[pl.ds(aligned(lax.rem(place + k, YS) * 40, 40), 40), :]


def sum_y_body(a, b, c, d, out):
    out[...] = (a[...] + b[...]) + (c[...] + d[...])


def add_body(a, b, out):
    out[...] = a[...] + b[...]


def join_y_body(index, a, b, c, d, gate_part, out):
    place = index[1] // ZS
    for k, part in enumerate((a, b, c, d)):
        origin = lax.rem(place + YS - k, YS)
        out[pl.ds(aligned(origin * 40, 40), 40), :] = part[...]
    out[160:176, :] = gate_part[...]


def join_x_body(index, a, b, c, d, out, slots):
    place = index[0] // 2
    for k, part in enumerate((a, b, c, d)):
        origin = lax.rem(place + XS - k, XS)
        out[pl.ds(aligned(origin * 160, 160), 160), :] = part[0:160, :]
        slots[origin] = part[160:176, :]
    out[640:656, :] = (slots[0] + slots[1]) + (slots[2] + slots[3])


def join_core_body(index, mine, other, *refs):
    outs, (inner, outer, total) = refs[:5], refs[5:]
    core = lax.rem(index[0], 2)
    total[pl.ds(aligned(core * 640, 640), 640), :] = mine[0:640, :]
    total[pl.ds(aligned((1 - core) * 640, 640), 640), :] = other[0:640, :]
    for k in range(5):
        outs[k][...] = total[k * 256 : (k + 1) * 256, :]
    gate = mine[640:656, :] + other[640:656, :]
    for k in range(2):
        rows = slice(16 * k, 16 * k + 16)
        inner[rows, :] = gate[:, 128 * k : 128 * k + 32]
        outer[rows, :] = gate[:, 128 * k + 32 : 128 * k + 64]


def exchange_seq(chunks):
    return [chunks[0]] + [
        lax.ppermute(chunks[i], "seq", [(s, (s + i) % SEQ) for s in range(SEQ)])
        for i in range(1, SEQ)
    ]


def swap_core(value):
    return lax.ppermute(value, "seq", [(s, s ^ 1) for s in range(SEQ)])


def shift_x(value, k):
    return lax.ppermute(value, "seq", [(s, (s + 2 * k) % SEQ) for s in range(SEQ)])


def shift_y(value, k):
    pairs = [(y * ZS + z, (y + k) % YS * ZS + z) for y in range(YS) for z in range(ZS)]
    return lax.ppermute(value, "dp", pairs)


def swap_dp(value, flip):
    return lax.ppermute(value, "dp", [(d, d ^ flip) for d in range(YS * ZS)])


def exchange_dp(value):
    return lax.all_to_all(value, "dp", 0, 0, tiled=True)


def per_device(
    inputs,
    cotangent,
    first_factor,
    second_sequence_factor,
    inverse_second_factor,
    inverse_first,
    twiddle,
    kernel,
    gate_inner,
    gate_outer,
):
    index = jnp.stack([lax.axis_index("seq"), lax.axis_index("dp")]).astype(jnp.int32)
    inner, outer = (gate_inner[0], whole_cut), (gate_outer[0], whole_cut)
    first, second, inverse_second, inverse_1st, twid, spectral = [
        (f, whole_cut)
        for f in (
            first_factor, second_sequence_factor, inverse_second_factor, inverse_first, twiddle, kernel
        )
    ]
    x, cot = (inputs, wide_cut), (cotangent, wide_cut)
    rows_out, wide_out, chan_out = (sds(*ROWS), rows_cut), (sds(*WIDE), wide_cut), (sds(*CHAN), whole_cut)
    vchan = pltpu.VMEM(CHAN, F32)
    small = 2 * 3 * 32 * 32 * 8192
    product = 2 * 3 * 1024 * 256 * 256

    (within,) = staged(within_body, [rows_out], [x, inner], flops=small, name="within")
    within_spread = exchange_dp(within)

    (x_chunks,) = staged(x_rows_body, [], [x], spreads=1, index=index, name="x_rows")
    x_chunks = exchange_seq(x_chunks)
    pre, spectrum, unmixed, mixed_chunks = staged(
        forward_body, [chan_out] * 3, [first, twid, second, spectral, inverse_second, inverse_1st],
        [x_chunks], 1, 1, index, scratch=[vchan], flops=4 * product, name="forward",
    )
    mixed_chunks = exchange_seq(mixed_chunks)

    (gate_spread,) = staged(
        gate_body, [rows_out], [(within_spread, rows_cut), outer], after=[pre], flops=small,
        name="gate",
    )
    gate = exchange_dp(gate_spread)
    (weighed,) = staged(weigh_body, [rows_out], [cot], [mixed_chunks], index=index, name="weigh")
    (across_grad,) = staged(
        across_grad_body, [rows_out], [(weighed, rows_cut), (gate, rows_cut)], name="across_grad"
    )
    across_grad_spread = exchange_dp(across_grad)
    (grad_chunks,) = staged(
        mixed_grad_body, [], [cot, (gate, rows_cut)], spreads=1, index=index, after=[across_grad],
        name="mixed_grad",
    )
    (output,) = staged(
        output_body, [wide_out], [x, (gate, rows_cut)], [mixed_chunks], index=index,
        after=[grad_chunks[0]], name="output",
    )
    grad_chunks = exchange_seq(grad_chunks)

    series, kernel_grad, keep, send = staged(
        backward_body,
        [chan_out, (sds(4, 256, 256), whole_cut)] + [(sds(640, 256), whole_cut)] * 2,
        [
            inverse_1st, (unmixed, whole_cut), inverse_second, spectral, (spectrum, whole_cut), second,
            twid, (pre, whole_cut), first,
        ],
        [grad_chunks, x_chunks], 0, 1, index, [output],
        [vchan, vchan, vchan, vchan, pltpu.VMEM((1280, 256), F32)],
        flops=8 * product, name="backward",
    )
    (within_grad_spread,) = staged(
        within_grad_body, [rows_out], [(across_grad_spread, rows_cut), outer], after=[keep],
        flops=small, name="within_grad",
    )
    within_grad = exchange_dp(within_grad_spread)
    got = swap_core(send)
    quarters = small_call(
        sum_core_body, [(160, 256)] * XS, [keep, got], [pltpu.VMEM((640, 256), F32)], index,
        [within_grad_spread], "sum_core",
    )
    quarters = [quarters[0]] + [shift_x(quarters[k], k) for k in range(1, XS)]
    parts = small_call(
        sum_x_body, [(40, 256)] * YS, quarters, [pltpu.VMEM((160, 256), F32)], index, name="sum_x"
    )
    parts = [parts[0]] + [shift_y(parts[k], k) for k in range(1, YS)]
    (part,) = small_call(sum_y_body, [(40, 256)], parts, name="sum_y")
    (series_rows,) = staged(
        series_body, [(sds(*ROWS), whole_cut)], [(series, whole_cut)], parts=1, index=index,
        after=[part], limit=NEAR, name="series_rows",
    )
    (part,) = small_call(add_body, [(40, 256)], [part, swap_dp(part, 1)], name="sum_z")
    got = swap_dp(part, 2)
    (outer_part,) = staged(
        outer_grad_body, [(sds(32, 32), None)],
        [(across_grad_spread, rows_cut), (within_spread, rows_cut)], after=[part], flops=small,
        limit=NEAR, name="outer_grad",
    )
    (part,) = small_call(add_body, [(40, 256)], [part, got], after=[outer_part], name="sum_z")
    series_rows = lax.all_to_all(series_rows, "seq", 0, 0, tiled=True)
    (part,) = small_call(add_body, [(40, 256)], [part, swap_dp(part, 4)], name="sum_z")
    (gate_part,) = staged(
        inner_grad_body, [(sds(16, 256), None)],
        [(within_grad, rows_cut), x, (outer_part, whole_cut)], after=[part],
        scratch=[pltpu.VMEM((32, 32), F32)], flops=small, limit=NEAR, name="inner_grad",
    )
    parts = [part] + [shift_y(part, k) for k in range(1, YS)]
    (part,) = small_call(
        join_y_body, [(176, 256)], parts + [gate_part], index=index, name="join_y"
    )
    (input_grad,) = staged(
        input_grad_body, [wide_out], [cot, (series_rows, rows_cut), (within_grad, rows_cut), inner],
        after=[part], flops=small, limit=NEAR, name="input_grad",
    )
    parts = [part] + [shift_x(part, k) for k in range(1, XS)]
    (half,) = small_call(
        join_x_body, [(656, 256)], parts, [pltpu.VMEM((XS, 16, 256), F32)], index,
        [input_grad], "join_x",
    )
    *totals, inner_total, outer_total = small_call(
        join_core_body, [(256, 256)] * 5 + [(32, 32)] * 2, [half, swap_core(half)],
        [pltpu.VMEM((1280, 256), F32)], index, name="join_core",
    )
    first_total, second_total, inverse_second_total, inverse_first_total, twiddle_total = totals
    return (
        output,
        input_grad,
        first_total,
        second_total,
        inverse_second_total,
        inverse_first_total,
        twiddle_total,
        kernel_grad,
        inner_total[None],
        outer_total[None],
    )


def solution(mesh):
    wide = P("dp", "seq")
    gate = P("dp", None, None)
    spectral = P(("dp", "seq"), None, None)
    return jax.shard_map(
        per_device,
        mesh=mesh,
        in_specs=(wide, wide, P(), P(), P(), P(), P(), spectral, gate, gate),
        out_specs=(wide, wide, P(), P(), P(), P(), P(), spectral, gate, gate),
        check_vma=False,
    )
```

```python
import functools

import jax
import jax.numpy as jnp
from jax import lax
from jax.experimental import pallas as pl
from jax.experimental.pallas import tpu as pltpu
from jax.sharding import PartitionSpec as P

F32 = jnp.float32
BF16 = jnp.bfloat16
MIB = 1024 * 1024

NN = (((1,), (0,)), ((), ()))
NT = (((1,), (1,)), ((), ()))
TN = (((0,), (0,)), ((), ()))

SEQ = 8
XS = 4
YS = 4
ZS = 8


def sds(*shape):
    return jax.ShapeDtypeStruct(shape, F32)


VMEM = pl.BlockSpec(memory_space=pltpu.VMEM)
SMEM = pl.BlockSpec(memory_space=pltpu.SMEM)
HBM = pl.BlockSpec(memory_space=pltpu.HBM)
ANY = pl.BlockSpec(memory_space=pl.ANY)

ROWS = (32, 64, 128)
CHUNK = (4, 64, 128)
WIDE = (32, 8192)
CHAN = (1024, 256)
FULL = int(63.7 * MIB)
NEAR = int(62.9 * MIB)
PARTS = 4
PAIRS = 64 // PARTS // 2


def wide_cut(p):
    return (slice(None), pl.ds(p * 2048, 2048))


def rows_cut(p):
    return (slice(None), pl.ds(p * 16, 16)) if p < PARTS else None


def whole_cut(p):
    return (slice(None),) if p == 0 else None


class Flow:
    def __init__(self):
        self.coming, self.leaving, self.sent = {}, {}, []

    def need(self, k):
        for c in self.coming.pop(k, []):
            c.wait()

    def flush(self, k):
        for c in self.leaving.pop(k, []):
            c.start()
            self.sent.append(c)


def staged(
    body, outs, args, gathers=(), spreads=0, parts=PARTS, index=None, after=(), scratch=(),
    flops=0, limit=FULL, name=None,
):
    n_in, n_out, n_after = len(args), len(outs), len(after)
    flat = [c for g in gathers for c in g]
    chunk_outs = [sds(*CHUNK)] * (SEQ * spreads)
    cut_in = [k for k in range(n_in) if args[k][1] is not None]
    cut_out = [k for k in range(n_out) if outs[k][1] is not None]

    def kernel(*refs):
        refs = list(refs)

        def take(n):
            taken = refs[:n]
            del refs[:n]
            return taken

        place = take(1)[0] if index is not None else None
        in_refs, chunk_refs, _ = take(n_in), take(len(flat)), take(n_after)
        out_refs, spread_refs = take(n_out), take(len(chunk_outs))
        in_bufs, gathered = take(len(cut_in)), take(len(gathers))
        out_bufs, spread = take(len(cut_out)), take(spreads)
        sems = take(1)[0]
        count = [0]

        def copy(source, target):
            made = pltpu.make_async_copy(source, target, sems.at[count[0]])
            count[0] += 1
            return made

        flow = Flow()
        ins, results = list(in_refs), list(out_refs)

        def gather(g):
            arriving = []
            for i in range(SEQ):
                at = pl.ds(lax.rem(place[0] + SEQ - i, SEQ) * 4, 4)
                arriving.append(copy(chunk_refs[g * SEQ + i], gathered[g].at[at]))
                arriving[-1].start()
            flow.coming["rows", g] = arriving

        if gathers:
            gather(0)
        for b, k in enumerate(cut_in):
            ins[k] = in_bufs[b]
        for p in range(parts):
            for b, k in enumerate(cut_in):
                at = args[k][1](p)
                if at is not None:
                    made = copy(in_refs[k].at[at], in_bufs[b].at[at])
                    made.start()
                    flow.coming.setdefault(k if parts == 1 else (k, p), []).append(made)
        for g in range(1, len(gathers)):
            gather(g)
        for b, k in enumerate(cut_out):
            results[k] = out_bufs[b]
            for p in range(parts):
                at = outs[k][1](p)
                if at is not None:
                    flow.leaving.setdefault(k if parts == 1 else (k, p), []).append(
                        copy(out_bufs[b].at[at], out_refs[k].at[at])
                    )
        for s in range(spreads):
            for p in range(parts):
                at = pl.ds(p * (64 // parts), 64 // parts)
                flow.leaving["rows", s, p] = [
                    copy(
                        spread[s].at[pl.ds(lax.rem(place[0] + i, SEQ) * 4, 4), at],
                        spread_refs[s * SEQ + i].at[:, at],
                    )
                    for i in range(SEQ)
                ]
        for p in range(parts):
            if parts > 1:
                for g in range(len(gathers)):
                    flow.need(("rows", g))
                for k in cut_in:
                    flow.need((k, p))
            body(p, flow, ins, gathered, results, spread, refs + [place])
            if parts > 1:
                for k in cut_out:
                    flow.flush((k, p))
                for s in range(spreads):
                    flow.flush(("rows", s, p))
        for k in list(flow.coming):
            flow.need(k)
        for k in list(flow.leaving):
            flow.flush(k)
        for c in flow.sent:
            c.wait()

    operands = [a for a, _ in args] + flat + list(after)
    specs = [VMEM if cut is None else ANY for _, cut in args] + [ANY] * (len(flat) + n_after)
    if index is not None:
        operands, specs = [index] + operands, [SMEM] + specs
    n_sems = len(cut_in) * parts + len(flat) + (len(cut_out) + len(chunk_outs)) * parts
    moved = sum(4 * a.size for a, _ in args) + sum(4 * o.size for o, _ in outs)
    moved += sum(4 * c.size for c in flat) + sum(4 * c.size for c in chunk_outs)
    buffers = [pltpu.VMEM(args[k][0].shape, F32) for k in cut_in]
    buffers += [pltpu.VMEM(ROWS, F32)] * len(gathers)
    buffers += [pltpu.VMEM(outs[k][0].shape, F32) for k in cut_out]
    buffers += [pltpu.VMEM(ROWS, F32)] * spreads
    result = list(
        pl.pallas_call(
            kernel,
            out_shape=[o for o, _ in outs] + chunk_outs,
            in_specs=specs,
            out_specs=[VMEM if cut is None else ANY for _, cut in outs] + [ANY] * len(chunk_outs),
            scratch_shapes=buffers + [pltpu.SemaphoreType.DMA((max(n_sems, 1),))] + list(scratch),
            compiler_params=pltpu.CompilerParams(vmem_limit_bytes=limit),
            cost_estimate=pl.CostEstimate(flops=flops, bytes_accessed=moved, transcendentals=0),
            name=name,
        )(*operands)
    )
    return result[:n_out] + [result[n_out + SEQ * s : n_out + SEQ * (s + 1)] for s in range(spreads)]


def hold(array, after):
    def kernel(*refs):
        del refs

    return pl.pallas_call(
        kernel,
        out_shape=jax.ShapeDtypeStruct(array.shape, array.dtype),
        in_specs=[ANY] * (1 + len(after)),
        out_specs=ANY,
        input_output_aliases={0: 0},
        compiler_params=pltpu.CompilerParams(vmem_limit_bytes=NEAR),
        name="hold",
    )(array, *after)


def small_call(body, outs, args, scratch=(), index=None, after=(), name=None):
    operands, specs, lead = list(args), [VMEM] * len(args), len(args)
    if index is not None:
        operands, specs, lead = [index] + operands, [SMEM] + specs, lead + 1

    def kernel(*refs):
        body(*refs[:lead], *refs[lead + len(after) :])

    return list(
        pl.pallas_call(
            kernel,
            out_shape=[sds(*o) for o in outs],
            in_specs=specs + [ANY] * len(after),
            out_specs=[VMEM] * len(outs),
            scratch_shapes=list(scratch),
            compiler_params=pltpu.CompilerParams(vmem_limit_bytes=8 * MIB),
            name=name,
        )(*operands, *after)
    )


def split(value):
    high = value.astype(BF16)
    return high, (value - high.astype(F32)).astype(BF16)


def dot3(left, right, form):
    (lh, ll), (rh, rl) = left, right
    dot = functools.partial(lax.dot_general, dimension_numbers=form, preferred_element_type=F32)
    return dot(lh, rh) + (dot(lh, rl) + dot(ll, rh))


def stack(weight):
    return jnp.concatenate(weight, axis=0), weight[0]


def mix(weight, block):
    both, high = weight
    dot = functools.partial(lax.dot_general, dimension_numbers=NN, preferred_element_type=F32)
    product = dot(both, block[0])
    return product[:32] + (dot(high, block[1]) + product[32:])


def aligned(offset, step):
    return pl.multiple_of(offset, step)


def pairs_of(p):
    return range(p * PAIRS, (p + 1) * PAIRS)


def columns(j):
    return slice(j * 256, (j + 1) * 256)


def get_rows(ref, j):
    return jnp.concatenate([ref[:, 2 * j, :], ref[:, 2 * j + 1, :]], axis=1)


def put_rows(ref, j, value):
    ref[:, 2 * j, :] = value[:, :128]
    ref[:, 2 * j + 1, :] = value[:, 128:]


def within_body(p, flow, ins, gathered, outs, spread, scratch):
    x, inner = ins
    weight = stack(split(inner[...]))
    for j in pairs_of(p):
        put_rows(outs[0], j, mix(weight, split(x[:, columns(j)])))


def x_rows_body(p, flow, ins, gathered, outs, spread, scratch):
    for j in pairs_of(p):
        put_rows(spread[0], j, ins[0][:, columns(j)])


def gate_body(p, flow, ins, gathered, outs, spread, scratch):
    within, outer = ins
    weight = stack(split(outer[...]))
    for j in pairs_of(p):
        put_rows(outs[0], j, jax.nn.sigmoid(mix(weight, split(get_rows(within, j)))))


def weigh_body(p, flow, ins, gathered, outs, spread, scratch):
    for j in pairs_of(p):
        put_rows(outs[0], j, ins[0][:, columns(j)] * get_rows(gathered[0], j))


def gate_grad_body(p, flow, ins, gathered, outs, spread, scratch):
    weighed, gate, cot = ins
    at = (slice(None), slice(p * 16, (p + 1) * 16))
    g = gate[at]
    outs[0][at] = weighed[at] * g * (1.0 - g)
    for j in pairs_of(p):
        put_rows(spread[0], j, cot[:, columns(j)] * get_rows(gate, j))


def output_body(p, flow, ins, gathered, outs, spread, scratch):
    x, gate = ins
    for j in pairs_of(p):
        outs[0][:, columns(j)] = x[:, columns(j)] + get_rows(gathered[0], j) * get_rows(gate, j)


def within_grad_body(p, flow, ins, gathered, outs, spread, scratch):
    across_grad, outer = ins
    weight = stack(split(outer[...].T))
    for j in pairs_of(p):
        put_rows(outs[0], j, mix(weight, split(get_rows(across_grad, j))))


def outer_grad_body(p, flow, ins, gathered, outs, spread, scratch):
    total = outs[0][...] if p else jnp.zeros((32, 32), F32)
    for j in pairs_of(p):
        total = total + dot3(split(get_rows(ins[0], j)), split(get_rows(ins[1], j)), NT)
    outs[0][...] = total


def inner_grad_body(p, flow, ins, gathered, outs, spread, scratch):
    within_grad, x, outer_part = ins
    held = scratch[0]
    total = held[...] if p else jnp.zeros((32, 32), F32)
    for j in pairs_of(p):
        total = total + dot3(split(get_rows(within_grad, j)), split(x[:, columns(j)]), NT)
    held[...] = total
    if p == PARTS - 1:
        out = outs[0]
        out[...] = jnp.zeros_like(out)
        for k in range(2):
            rows = slice(16 * k, 16 * k + 16)
            out[:, 128 * k : 128 * k + 32] = held[rows, :]
            out[:, 128 * k + 32 : 128 * k + 64] = outer_part[rows, :]


def input_grad_body(p, flow, ins, gathered, outs, spread, scratch):
    cot, series, within_grad, inner = ins
    weight = stack(split(inner[...].T))
    for j in pairs_of(p):
        product = mix(weight, split(get_rows(within_grad, j)))
        outs[0][:, columns(j)] = (cot[:, columns(j)] + get_rows(series, j)) + product


def assemble(c, chunks, out, start):
    for s in range(SEQ):
        at = slice(start + s * 32, start + (s + 1) * 32)
        out[at, 0:128] = chunks[s * 4 + c, pl.ds(0, 32, stride=2), :]
        out[at, 128:256] = chunks[s * 4 + c, pl.ds(1, 32, stride=2), :]


def disperse(c, value, chunks):
    for s in range(SEQ):
        rows = value[s * 32 : (s + 1) * 32, :]
        chunks[s * 4 + c, pl.ds(0, 32, stride=2), :] = rows[:, :128]
        chunks[s * 4 + c, pl.ds(1, 32, stride=2), :] = rows[:, 128:]


def channel(c):
    return slice(c * 256, (c + 1) * 256)


def forward_body(p, flow, ins, gathered, outs, spread, scratch):
    first, twiddle, second, kernel, inverse_second, inverse_first = ins
    pre, spectrum, unmixed = outs
    x = scratch[0]
    flow.need(("rows", 0))
    flow.need(0)
    weight = split(first[...])
    for c in range(4):
        assemble(c, gathered[0], x, c * 256)
        pre[channel(c), :] = dot3(split(x[channel(c), :]), weight, NT)
    flow.flush(0)
    flow.need(1)
    flow.need(2)
    weight = split(second[...])
    for c in range(4):
        spectrum[channel(c), :] = dot3(weight, split(twiddle[...] * pre[channel(c), :]), NN)
    flow.flush(1)
    flow.need(3)
    flow.need(4)
    weight = split(inverse_second[...])
    for c in range(4):
        unmixed[channel(c), :] = dot3(weight, split(kernel[c].T * spectrum[channel(c), :]), NN)
    flow.flush(2)
    flow.need(5)
    weight = split(inverse_first[...])
    for c in range(4):
        disperse(c, dot3(split(unmixed[channel(c), :]), weight, NT), spread[0])


def add_up(terms):
    total = terms[0]
    for term in terms[1:]:
        total = total + term
    return total


def backward_body(p, flow, ins, gathered, outs, spread, scratch):
    inverse_first, unmixed, inverse_second, kernel, spectrum, second, twiddle, pre, first = ins
    series, kernel_grad, keep, send = outs
    x, mixed_grad, work, unmixed_grad, total, place = scratch
    flow.need(("rows", 0))
    flow.need(0)
    weight = split(inverse_first[...])
    for c in range(4):
        assemble(c, gathered[0], mixed_grad, c * 256)
        unmixed_grad[channel(c), :] = dot3(split(mixed_grad[channel(c), :]), weight, NN)
    flow.need(1)
    total[768:1024, :] = dot3(split(mixed_grad[...]), split(unmixed[...]), TN)
    flow.need(2)
    flow.need(3)
    flow.need(4)
    weight = split(inverse_second[...].T)
    terms = []
    for c in range(4):
        du = split(unmixed_grad[channel(c), :])
        kt = kernel[c].T
        sp = spectrum[channel(c), :]
        dsc = dot3(weight, du, NN)
        kernel_grad[c] = (dsc * sp).T
        work[channel(c), :] = dsc * kt
        terms.append(dot3(du, split(kt * sp), NT))
    total[512:768, :] = add_up(terms)
    flow.flush(1)
    flow.need(5)
    flow.need(6)
    flow.need(7)
    weight = split(second[...].T)
    terms, twiddles = [], []
    for c in range(4):
        dsp = split(work[channel(c), :])
        ds = dot3(weight, dsp, NN)
        product = pre[channel(c), :]
        terms.append(dot3(dsp, split(twiddle[...] * product), NT))
        twiddles.append(ds * product)
        mixed_grad[channel(c), :] = ds * twiddle[...]
    total[256:512, :] = add_up(terms)
    total[1024:1280, :] = add_up(twiddles)
    flow.need(("rows", 1))
    flow.need(8)
    weight = split(first[...])
    for c in range(4):
        assemble(c, gathered[1], x, c * 256)
        disperse(c, dot3(split(mixed_grad[channel(c), :]), weight, NN), series)
    flow.flush(0)
    total[0:256, :] = dot3(split(mixed_grad[...]), split(x[...]), TN)
    core = lax.rem(place[0], 2)
    keep[...] = total[pl.ds(aligned(core * 640, 640), 640), :]
    send[...] = total[pl.ds(aligned((1 - core) * 640, 640), 640), :]


def sum_core_body(index, keep, got, *refs):
    outs, total = refs[:XS], refs[XS]
    total[...] = keep[...] + got[...]
    place = index[0] // 2
    for k in range(XS):
        outs[k][...] = total[pl.ds(aligned(lax.rem(place + k, XS) * 160, 160), 160), :]


def sum_x_body(index, a, b, c, d, *refs):
    outs, total = refs[:YS], refs[YS]
    total[...] = (a[...] + b[...]) + (c[...] + d[...])
    place = index[1] // ZS
    for k in range(YS):
        outs[k][...] = total[pl.ds(aligned(lax.rem(place + k, YS) * 40, 40), 40), :]


def sum_y_body(a, b, c, d, out):
    out[...] = (a[...] + b[...]) + (c[...] + d[...])


def add_body(a, b, out):
    out[...] = a[...] + b[...]


def join_y_body(index, a, b, c, d, gate_part, out):
    place = index[1] // ZS
    for k, part in enumerate((a, b, c, d)):
        origin = lax.rem(place + YS - k, YS)
        out[pl.ds(aligned(origin * 40, 40), 40), :] = part[...]
    out[160:176, :] = gate_part[...]


def join_x_body(index, a, b, c, d, out, slots):
    place = index[0] // 2
    for k, part in enumerate((a, b, c, d)):
        origin = lax.rem(place + XS - k, XS)
        out[pl.ds(aligned(origin * 160, 160), 160), :] = part[0:160, :]
        slots[origin] = part[160:176, :]
    out[640:656, :] = (slots[0] + slots[1]) + (slots[2] + slots[3])


def join_core_body(index, mine, other, *refs):
    outs, (inner, outer, total) = refs[:5], refs[5:]
    core = lax.rem(index[0], 2)
    total[pl.ds(aligned(core * 640, 640), 640), :] = mine[0:640, :]
    total[pl.ds(aligned((1 - core) * 640, 640), 640), :] = other[0:640, :]
    for k in range(5):
        outs[k][...] = total[k * 256 : (k + 1) * 256, :]
    gate = mine[640:656, :] + other[640:656, :]
    for k in range(2):
        rows = slice(16 * k, 16 * k + 16)
        inner[rows, :] = gate[:, 128 * k : 128 * k + 32]
        outer[rows, :] = gate[:, 128 * k + 32 : 128 * k + 64]


def exchange_seq(chunks):
    return [chunks[0]] + [
        lax.ppermute(chunks[i], "seq", [(s, (s + i) % SEQ) for s in range(SEQ)])
        for i in range(1, SEQ)
    ]


def swap_core(value):
    return lax.ppermute(value, "seq", [(s, s ^ 1) for s in range(SEQ)])


def shift_x(value, k):
    return lax.ppermute(value, "seq", [(s, (s + 2 * k) % SEQ) for s in range(SEQ)])


def shift_y(value, k):
    pairs = [(y * ZS + z, (y + k) % YS * ZS + z) for y in range(YS) for z in range(ZS)]
    return lax.ppermute(value, "dp", pairs)


def swap_dp(value, flip):
    return lax.ppermute(value, "dp", [(d, d ^ flip) for d in range(YS * ZS)])


def exchange_dp(value):
    return lax.all_to_all(value, "dp", 0, 0, tiled=True)


def per_device(
    inputs,
    cotangent,
    first_factor,
    second_sequence_factor,
    inverse_second_factor,
    inverse_first,
    twiddle,
    kernel,
    gate_inner,
    gate_outer,
):
    index = jnp.stack([lax.axis_index("seq"), lax.axis_index("dp")]).astype(jnp.int32)
    inner, outer = (gate_inner[0], whole_cut), (gate_outer[0], whole_cut)
    first, second, inverse_second, inverse_1st, twid, spectral = [
        (f, whole_cut)
        for f in (
            first_factor, second_sequence_factor, inverse_second_factor, inverse_first, twiddle, kernel
        )
    ]
    x, cot = (inputs, wide_cut), (cotangent, wide_cut)
    rows_out, wide_out, chan_out = (sds(*ROWS), rows_cut), (sds(*WIDE), wide_cut), (sds(*CHAN), whole_cut)
    vchan = pltpu.VMEM(CHAN, F32)
    small = 2 * 3 * 32 * 32 * 8192
    product = 2 * 3 * 1024 * 256 * 256

    (within,) = staged(within_body, [rows_out], [x, inner], flops=small, name="within")
    within_spread = exchange_dp(within)

    (x_chunks,) = staged(x_rows_body, [], [x], spreads=1, index=index, name="x_rows")
    x_chunks = exchange_seq(x_chunks)
    pre, spectrum, unmixed, mixed_chunks = staged(
        forward_body, [chan_out] * 3, [first, twid, second, spectral, inverse_second, inverse_1st],
        [x_chunks], 1, 1, index, scratch=[vchan], flops=4 * product, name="forward",
    )
    mixed_chunks = exchange_seq(mixed_chunks)

    (gate_spread,) = staged(
        gate_body, [rows_out], [(within_spread, rows_cut), outer], after=[pre], flops=small,
        name="gate",
    )
    gate = exchange_dp(gate_spread)
    (weighed,) = staged(weigh_body, [rows_out], [cot], [mixed_chunks], index=index, name="weigh")
    across_grad, grad_chunks = staged(
        gate_grad_body, [rows_out], [(weighed, rows_cut), (gate, rows_cut), cot], spreads=1,
        index=index, name="gate_grad",
    )
    across_grad_spread = exchange_dp(across_grad)
    (output,) = staged(
        output_body, [wide_out], [x, (gate, rows_cut)], [mixed_chunks], index=index,
        after=[grad_chunks[0]], name="output",
    )
    grad_chunks = exchange_seq(grad_chunks)

    series, kernel_grad, keep, send = staged(
        backward_body,
        [(sds(*ROWS), whole_cut), (sds(4, 256, 256), whole_cut)] + [(sds(640, 256), whole_cut)] * 2,
        [
            inverse_1st, (unmixed, whole_cut), inverse_second, spectral, (spectrum, whole_cut), second,
            twid, (pre, whole_cut), first,
        ],
        [grad_chunks, x_chunks], 0, 1, index, [output],
        [vchan, vchan, vchan, vchan, pltpu.VMEM((1280, 256), F32)],
        flops=8 * product, name="backward",
    )
    quarters = small_call(
        sum_core_body, [(160, 256)] * XS, [keep, swap_core(send)], [pltpu.VMEM((640, 256), F32)],
        index, name="sum_core",
    )
    (within_grad_spread,) = staged(
        within_grad_body, [rows_out], [(across_grad_spread, rows_cut), outer], after=[quarters[0]],
        flops=small, limit=NEAR, name="within_grad",
    )
    within_grad = exchange_dp(within_grad_spread)
    (outer_part,) = staged(
        outer_grad_body, [(sds(32, 32), None)],
        [(across_grad_spread, rows_cut), (within_spread, rows_cut)], after=[within_grad_spread],
        flops=small, limit=NEAR, name="outer_grad",
    )
    quarters = [quarters[0]] + [shift_x(quarters[k], k) for k in range(1, XS)]
    parts = small_call(
        sum_x_body, [(40, 256)] * YS, quarters, [pltpu.VMEM((160, 256), F32)], index, [outer_part],
        "sum_x",
    )
    parts = [parts[0]] + [shift_y(parts[k], k) for k in range(1, YS)]
    (part,) = small_call(sum_y_body, [(40, 256)], parts, name="sum_y")
    for flip in (1, 2):
        (part,) = small_call(add_body, [(40, 256)], [part, swap_dp(part, flip)], name="sum_z")
    series = lax.all_to_all(hold(series, [part]), "seq", 0, 0, tiled=True)
    (part,) = small_call(add_body, [(40, 256)], [part, swap_dp(part, 4)], name="sum_z")
    (gate_part,) = staged(
        inner_grad_body, [(sds(16, 256), None)],
        [(within_grad, rows_cut), x, (outer_part, whole_cut)], after=[part],
        scratch=[pltpu.VMEM((32, 32), F32)], flops=small, limit=NEAR, name="inner_grad",
    )
    parts = [part] + [shift_y(part, k) for k in range(1, YS)]
    (part,) = small_call(
        join_y_body, [(176, 256)], parts + [gate_part], index=index, name="join_y"
    )
    (input_grad,) = staged(
        input_grad_body, [wide_out],
        [cot, (series, rows_cut), (within_grad, rows_cut), inner], after=[part], flops=small,
        limit=NEAR, name="input_grad",
    )
    parts = [part] + [shift_x(part, k) for k in range(1, XS)]
    (half,) = small_call(
        join_x_body, [(656, 256)], parts, [pltpu.VMEM((XS, 16, 256), F32)],
        hold(index, [input_grad]), name="join_x",
    )
    *totals, inner_total, outer_total = small_call(
        join_core_body, [(256, 256)] * 5 + [(32, 32)] * 2, [half, swap_core(half)],
        [pltpu.VMEM((1280, 256), F32)], index, name="join_core",
    )
    first_total, second_total, inverse_second_total, inverse_first_total, twiddle_total = totals
    return (
        output,
        input_grad,
        first_total,
        second_total,
        inverse_second_total,
        inverse_first_total,
        twiddle_total,
        kernel_grad,
        inner_total[None],
        outer_total[None],
    )


def solution(mesh):
    wide = P("dp", "seq")
    gate = P("dp", None, None)
    spectral = P(("dp", "seq"), None, None)
    return jax.shard_map(
        per_device,
        mesh=mesh,
        in_specs=(wide, wide, P(), P(), P(), P(), P(), spectral, gate, gate),
        out_specs=(wide, wide, P(), P(), P(), P(), P(), spectral, gate, gate),
        check_vma=False,
    )
```

```python
import functools

import jax
import jax.numpy as jnp
from jax import lax
from jax.experimental import pallas as pl
from jax.experimental.pallas import tpu as pltpu
from jax.sharding import PartitionSpec as P

F32 = jnp.float32
BF16 = jnp.bfloat16
MIB = 1024 * 1024

NN = (((1,), (0,)), ((), ()))
NT = (((1,), (1,)), ((), ()))
TN = (((0,), (0,)), ((), ()))

SEQ = 8
XS = 4
YS = 4
ZS = 8


def sds(*shape):
    return jax.ShapeDtypeStruct(shape, F32)


VMEM = pl.BlockSpec(memory_space=pltpu.VMEM)
SMEM = pl.BlockSpec(memory_space=pltpu.SMEM)
HBM = pl.BlockSpec(memory_space=pltpu.HBM)
ANY = pl.BlockSpec(memory_space=pl.ANY)

ROWS = (32, 64, 128)
CHUNK = (4, 64, 128)
WIDE = (32, 8192)
CHAN = (1024, 256)
FULL = int(63.7 * MIB)
NEAR = int(62.9 * MIB)
PARTS = 4
PAIRS = 64 // PARTS // 2


def wide_cut(p):
    return (slice(None), pl.ds(p * 2048, 2048))


def rows_cut(p):
    return (slice(None), pl.ds(p * 16, 16)) if p < PARTS else None


def whole_cut(p):
    return (slice(None),) if p == 0 else None


class Flow:
    def __init__(self):
        self.coming, self.leaving, self.sent = {}, {}, []

    def need(self, k):
        for c in self.coming.pop(k, []):
            c.wait()

    def flush(self, k):
        for c in self.leaving.pop(k, []):
            c.start()
            self.sent.append(c)


def staged(
    body, outs, args, gathers=(), spreads=0, parts=PARTS, index=None, after=(), scratch=(),
    flops=0, limit=FULL, name=None,
):
    n_in, n_out, n_after = len(args), len(outs), len(after)
    flat = [c for g in gathers for c in g]
    chunk_outs = [sds(*CHUNK)] * (SEQ * spreads)
    cut_in = [k for k in range(n_in) if args[k][1] is not None]
    cut_out = [k for k in range(n_out) if outs[k][1] is not None]

    def kernel(*refs):
        refs = list(refs)

        def take(n):
            taken = refs[:n]
            del refs[:n]
            return taken

        place = take(1)[0] if index is not None else None
        in_refs, chunk_refs, _ = take(n_in), take(len(flat)), take(n_after)
        out_refs, spread_refs = take(n_out), take(len(chunk_outs))
        in_bufs, gathered = take(len(cut_in)), take(len(gathers))
        out_bufs, spread = take(len(cut_out)), take(spreads)
        sems = take(1)[0]
        count = [0]

        def copy(source, target):
            made = pltpu.make_async_copy(source, target, sems.at[count[0]])
            count[0] += 1
            return made

        flow = Flow()
        ins, results = list(in_refs), list(out_refs)

        def gather(g):
            arriving = []
            for i in range(SEQ):
                at = pl.ds(lax.rem(place[0] + SEQ - i, SEQ) * 4, 4)
                arriving.append(copy(chunk_refs[g * SEQ + i], gathered[g].at[at]))
                arriving[-1].start()
            flow.coming["rows", g] = arriving

        if gathers:
            gather(0)
        for b, k in enumerate(cut_in):
            ins[k] = in_bufs[b]
        for p in range(parts):
            for b, k in enumerate(cut_in):
                at = args[k][1](p)
                if at is not None:
                    made = copy(in_refs[k].at[at], in_bufs[b].at[at])
                    made.start()
                    flow.coming.setdefault(k if parts == 1 else (k, p), []).append(made)
        for g in range(1, len(gathers)):
            gather(g)
        for b, k in enumerate(cut_out):
            results[k] = out_bufs[b]
            for p in range(parts):
                at = outs[k][1](p)
                if at is not None:
                    flow.leaving.setdefault(k if parts == 1 else (k, p), []).append(
                        copy(out_bufs[b].at[at], out_refs[k].at[at])
                    )
        for s in range(spreads):
            for p in range(parts):
                at = pl.ds(p * (64 // parts), 64 // parts)
                flow.leaving["rows", s, p] = [
                    copy(
                        spread[s].at[pl.ds(lax.rem(place[0] + i, SEQ) * 4, 4), at],
                        spread_refs[s * SEQ + i].at[:, at],
                    )
                    for i in range(SEQ)
                ]
        for p in range(parts):
            if parts > 1:
                for g in range(len(gathers)):
                    flow.need(("rows", g))
                for k in cut_in:
                    flow.need((k, p))
            body(p, flow, ins, gathered, results, spread, refs + [place])
            if parts > 1:
                for k in cut_out:
                    flow.flush((k, p))
                for s in range(spreads):
                    flow.flush(("rows", s, p))
        for k in list(flow.coming):
            flow.need(k)
        for k in list(flow.leaving):
            flow.flush(k)
        for c in flow.sent:
            c.wait()

    operands = [a for a, _ in args] + flat + list(after)
    specs = [VMEM if cut is None else ANY for _, cut in args] + [ANY] * (len(flat) + n_after)
    if index is not None:
        operands, specs = [index] + operands, [SMEM] + specs
    n_sems = len(cut_in) * parts + len(flat) + (len(cut_out) + len(chunk_outs)) * parts
    moved = sum(4 * a.size for a, _ in args) + sum(4 * o.size for o, _ in outs)
    moved += sum(4 * c.size for c in flat) + sum(4 * c.size for c in chunk_outs)
    buffers = [pltpu.VMEM(args[k][0].shape, F32) for k in cut_in]
    buffers += [pltpu.VMEM(ROWS, F32)] * len(gathers)
    buffers += [pltpu.VMEM(outs[k][0].shape, F32) for k in cut_out]
    buffers += [pltpu.VMEM(ROWS, F32)] * spreads
    result = list(
        pl.pallas_call(
            kernel,
            out_shape=[o for o, _ in outs] + chunk_outs,
            in_specs=specs,
            out_specs=[VMEM if cut is None else ANY for _, cut in outs] + [ANY] * len(chunk_outs),
            scratch_shapes=buffers + [pltpu.SemaphoreType.DMA((max(n_sems, 1),))] + list(scratch),
            compiler_params=pltpu.CompilerParams(vmem_limit_bytes=limit),
            cost_estimate=pl.CostEstimate(flops=flops, bytes_accessed=moved, transcendentals=0),
            name=name,
        )(*operands)
    )
    return result[:n_out] + [result[n_out + SEQ * s : n_out + SEQ * (s + 1)] for s in range(spreads)]


def hold(array, after):
    def kernel(*refs):
        del refs

    return pl.pallas_call(
        kernel,
        out_shape=jax.ShapeDtypeStruct(array.shape, array.dtype),
        in_specs=[ANY] * (1 + len(after)),
        out_specs=ANY,
        input_output_aliases={0: 0},
        compiler_params=pltpu.CompilerParams(vmem_limit_bytes=NEAR),
        name="hold",
    )(array, *after)


def small_call(body, outs, args, scratch=(), index=None, after=(), name=None):
    operands, specs, lead = list(args), [VMEM] * len(args), len(args)
    if index is not None:
        operands, specs, lead = [index] + operands, [SMEM] + specs, lead + 1

    def kernel(*refs):
        body(*refs[:lead], *refs[lead + len(after) :])

    return list(
        pl.pallas_call(
            kernel,
            out_shape=[sds(*o) for o in outs],
            in_specs=specs + [ANY] * len(after),
            out_specs=[VMEM] * len(outs),
            scratch_shapes=list(scratch),
            compiler_params=pltpu.CompilerParams(vmem_limit_bytes=8 * MIB),
            name=name,
        )(*operands, *after)
    )


def split(value):
    high = value.astype(BF16)
    return high, (value - high.astype(F32)).astype(BF16)


def dot3(left, right, form):
    (lh, ll), (rh, rl) = left, right
    dot = functools.partial(lax.dot_general, dimension_numbers=form, preferred_element_type=F32)
    return dot(lh, rh) + (dot(lh, rl) + dot(ll, rh))


def stack(weight):
    return jnp.concatenate(weight, axis=0), weight[0]


def mix(weight, block):
    both, high = weight
    dot = functools.partial(lax.dot_general, dimension_numbers=NN, preferred_element_type=F32)
    product = dot(both, block[0])
    return product[:32] + (dot(high, block[1]) + product[32:])


def aligned(offset, step):
    return pl.multiple_of(offset, step)


def pairs_of(p):
    return range(p * PAIRS, (p + 1) * PAIRS)


def columns(j):
    return slice(j * 256, (j + 1) * 256)


def get_rows(ref, j):
    return jnp.concatenate([ref[:, 2 * j, :], ref[:, 2 * j + 1, :]], axis=1)


def put_rows(ref, j, value):
    ref[:, 2 * j, :] = value[:, :128]
    ref[:, 2 * j + 1, :] = value[:, 128:]


def within_body(p, flow, ins, gathered, outs, spread, scratch):
    x, inner = ins
    weight = stack(split(inner[...]))
    for j in pairs_of(p):
        put_rows(outs[0], j, mix(weight, split(x[:, columns(j)])))


def x_rows_body(p, flow, ins, gathered, outs, spread, scratch):
    for j in pairs_of(p):
        put_rows(spread[0], j, ins[0][:, columns(j)])


def gate_body(p, flow, ins, gathered, outs, spread, scratch):
    within, outer = ins
    weight = stack(split(outer[...]))
    for j in pairs_of(p):
        put_rows(outs[0], j, jax.nn.sigmoid(mix(weight, split(get_rows(within, j)))))


def weigh_body(p, flow, ins, gathered, outs, spread, scratch):
    for j in pairs_of(p):
        put_rows(outs[0], j, ins[0][:, columns(j)] * get_rows(gathered[0], j))


def gate_grad_body(p, flow, ins, gathered, outs, spread, scratch):
    weighed, gate, cot = ins
    at = (slice(None), slice(p * 16, (p + 1) * 16))
    g = gate[at]
    outs[0][at] = weighed[at] * g * (1.0 - g)
    for j in pairs_of(p):
        put_rows(spread[0], j, cot[:, columns(j)] * get_rows(gate, j))


def output_body(p, flow, ins, gathered, outs, spread, scratch):
    x, gate = ins
    for j in pairs_of(p):
        outs[0][:, columns(j)] = x[:, columns(j)] + get_rows(gathered[0], j) * get_rows(gate, j)


def within_grad_body(p, flow, ins, gathered, outs, spread, scratch):
    across_grad, outer = ins
    weight = stack(split(outer[...].T))
    for j in pairs_of(p):
        put_rows(outs[0], j, mix(weight, split(get_rows(across_grad, j))))


def outer_grad_body(p, flow, ins, gathered, outs, spread, scratch):
    total = outs[0][...] if p else jnp.zeros((32, 32), F32)
    for j in pairs_of(p):
        total = total + dot3(split(get_rows(ins[0], j)), split(get_rows(ins[1], j)), NT)
    outs[0][...] = total


def inner_grad_body(p, flow, ins, gathered, outs, spread, scratch):
    within_grad, x, outer_part = ins
    held = scratch[0]
    total = held[...] if p else jnp.zeros((32, 32), F32)
    for j in pairs_of(p):
        total = total + dot3(split(get_rows(within_grad, j)), split(x[:, columns(j)]), NT)
    held[...] = total
    if p == PARTS - 1:
        out = outs[0]
        out[...] = jnp.zeros_like(out)
        for k in range(2):
            rows = slice(16 * k, 16 * k + 16)
            out[:, 128 * k : 128 * k + 32] = held[rows, :]
            out[:, 128 * k + 32 : 128 * k + 64] = outer_part[rows, :]


def input_grad_body(p, flow, ins, gathered, outs, spread, scratch):
    cot, series, within_grad, inner = ins
    weight = stack(split(inner[...].T))
    for j in pairs_of(p):
        product = mix(weight, split(get_rows(within_grad, j)))
        outs[0][:, columns(j)] = (cot[:, columns(j)] + get_rows(series, j)) + product


def assemble(c, chunks, out, start):
    for s in range(SEQ):
        at = slice(start + s * 32, start + (s + 1) * 32)
        out[at, 0:128] = chunks[s * 4 + c, pl.ds(0, 32, stride=2), :]
        out[at, 128:256] = chunks[s * 4 + c, pl.ds(1, 32, stride=2), :]


def disperse(c, value, chunks):
    for s in range(SEQ):
        rows = value[s * 32 : (s + 1) * 32, :]
        chunks[s * 4 + c, pl.ds(0, 32, stride=2), :] = rows[:, :128]
        chunks[s * 4 + c, pl.ds(1, 32, stride=2), :] = rows[:, 128:]


def channel(c):
    return slice(c * 256, (c + 1) * 256)


def forward_body(p, flow, ins, gathered, outs, spread, scratch):
    first, twiddle, second, kernel, inverse_second, inverse_first = ins
    pre, spectrum, unmixed = outs
    x = scratch[0]
    flow.need(("rows", 0))
    flow.need(0)
    weight = split(first[...])
    for c in range(4):
        assemble(c, gathered[0], x, c * 256)
        pre[channel(c), :] = dot3(split(x[channel(c), :]), weight, NT)
    flow.flush(0)
    flow.need(1)
    flow.need(2)
    weight = split(second[...])
    for c in range(4):
        spectrum[channel(c), :] = dot3(weight, split(twiddle[...] * pre[channel(c), :]), NN)
    flow.flush(1)
    flow.need(3)
    flow.need(4)
    weight = split(inverse_second[...])
    for c in range(4):
        unmixed[channel(c), :] = dot3(weight, split(kernel[c].T * spectrum[channel(c), :]), NN)
    flow.flush(2)
    flow.need(5)
    weight = split(inverse_first[...])
    for c in range(4):
        disperse(c, dot3(split(unmixed[channel(c), :]), weight, NT), spread[0])


def add_up(terms):
    total = terms[0]
    for term in terms[1:]:
        total = total + term
    return total


def backward_body(p, flow, ins, gathered, outs, spread, scratch):
    inverse_first, unmixed, inverse_second, kernel, spectrum, second, twiddle, pre, first = ins
    series, kernel_grad, keep, send = outs
    x, mixed_grad, work, unmixed_grad, total, place = scratch
    flow.need(("rows", 0))
    flow.need(0)
    weight = split(inverse_first[...])
    for c in range(4):
        assemble(c, gathered[0], mixed_grad, c * 256)
        unmixed_grad[channel(c), :] = dot3(split(mixed_grad[channel(c), :]), weight, NN)
    flow.need(1)
    total[768:1024, :] = dot3(split(mixed_grad[...]), split(unmixed[...]), TN)
    flow.need(2)
    flow.need(3)
    flow.need(4)
    weight = split(inverse_second[...].T)
    terms = []
    for c in range(4):
        du = split(unmixed_grad[channel(c), :])
        kt = kernel[c].T
        sp = spectrum[channel(c), :]
        dsc = dot3(weight, du, NN)
        kernel_grad[c] = (dsc * sp).T
        work[channel(c), :] = dsc * kt
        terms.append(dot3(du, split(kt * sp), NT))
    total[512:768, :] = add_up(terms)
    flow.flush(1)
    flow.need(5)
    flow.need(6)
    flow.need(7)
    weight = split(second[...].T)
    terms, twiddles = [], []
    for c in range(4):
        dsp = split(work[channel(c), :])
        ds = dot3(weight, dsp, NN)
        product = pre[channel(c), :]
        terms.append(dot3(dsp, split(twiddle[...] * product), NT))
        twiddles.append(ds * product)
        mixed_grad[channel(c), :] = ds * twiddle[...]
    total[256:512, :] = add_up(terms)
    total[1024:1280, :] = add_up(twiddles)
    flow.need(("rows", 1))
    flow.need(8)
    weight = split(first[...])
    for c in range(4):
        assemble(c, gathered[1], x, c * 256)
        disperse(c, dot3(split(mixed_grad[channel(c), :]), weight, NN), series)
    flow.flush(0)
    total[0:256, :] = dot3(split(mixed_grad[...]), split(x[...]), TN)
    core = lax.rem(place[0], 2)
    keep[...] = total[pl.ds(aligned(core * 640, 640), 640), :]
    send[...] = total[pl.ds(aligned((1 - core) * 640, 640), 640), :]


def sum_core_body(index, keep, got, *refs):
    outs, total = refs[:XS], refs[XS]
    total[...] = keep[...] + got[...]
    place = index[0] // 2
    for k in range(XS):
        outs[k][...] = total[pl.ds(aligned(lax.rem(place + k, XS) * 160, 160), 160), :]


def sum_x_body(index, a, b, c, d, *refs):
    outs, total = refs[:YS], refs[YS]
    total[...] = (a[...] + b[...]) + (c[...] + d[...])
    place = index[1] // ZS
    for k in range(YS):
        outs[k][...] = total[pl.ds(aligned(lax.rem(place + k, YS) * 40, 40), 40), :]


def sum_y_body(a, b, c, d, out):
    out[...] = (a[...] + b[...]) + (c[...] + d[...])


def add_body(a, b, out):
    out[...] = a[...] + b[...]


def join_y_body(index, a, b, c, d, gate_part, out):
    place = index[1] // ZS
    for k, part in enumerate((a, b, c, d)):
        origin = lax.rem(place + YS - k, YS)
        out[pl.ds(aligned(origin * 40, 40), 40), :] = part[...]
    out[160:176, :] = gate_part[...]


def join_x_body(index, a, b, c, d, out, slots):
    place = index[0] // 2
    for k, part in enumerate((a, b, c, d)):
        origin = lax.rem(place + XS - k, XS)
        out[pl.ds(aligned(origin * 160, 160), 160), :] = part[0:160, :]
        slots[origin] = part[160:176, :]
    out[640:656, :] = (slots[0] + slots[1]) + (slots[2] + slots[3])


def join_core_body(index, mine, other, *refs):
    outs, (inner, outer, total) = refs[:5], refs[5:]
    core = lax.rem(index[0], 2)
    total[pl.ds(aligned(core * 640, 640), 640), :] = mine[0:640, :]
    total[pl.ds(aligned((1 - core) * 640, 640), 640), :] = other[0:640, :]
    for k in range(5):
        outs[k][...] = total[k * 256 : (k + 1) * 256, :]
    gate = mine[640:656, :] + other[640:656, :]
    for k in range(2):
        rows = slice(16 * k, 16 * k + 16)
        inner[rows, :] = gate[:, 128 * k : 128 * k + 32]
        outer[rows, :] = gate[:, 128 * k + 32 : 128 * k + 64]


def exchange_seq(chunks):
    return [chunks[0]] + [
        lax.ppermute(chunks[i], "seq", [(s, (s + i) % SEQ) for s in range(SEQ)])
        for i in range(1, SEQ)
    ]


def swap_core(value):
    return lax.ppermute(value, "seq", [(s, s ^ 1) for s in range(SEQ)])


def shift_x(value, k):
    return lax.ppermute(value, "seq", [(s, (s + 2 * k) % SEQ) for s in range(SEQ)])


def shift_y(value, k):
    pairs = [(y * ZS + z, (y + k) % YS * ZS + z) for y in range(YS) for z in range(ZS)]
    return lax.ppermute(value, "dp", pairs)


def swap_dp(value, flip):
    return lax.ppermute(value, "dp", [(d, d ^ flip) for d in range(YS * ZS)])


def exchange_dp(value):
    return lax.all_to_all(value, "dp", 0, 0, tiled=True)


def per_device(
    inputs,
    cotangent,
    first_factor,
    second_sequence_factor,
    inverse_second_factor,
    inverse_first,
    twiddle,
    kernel,
    gate_inner,
    gate_outer,
):
    index = jnp.stack([lax.axis_index("seq"), lax.axis_index("dp")]).astype(jnp.int32)
    inner, outer = (gate_inner[0], whole_cut), (gate_outer[0], whole_cut)
    first, second, inverse_second, inverse_1st, twid, spectral = [
        (f, whole_cut)
        for f in (
            first_factor, second_sequence_factor, inverse_second_factor, inverse_first, twiddle, kernel
        )
    ]
    x, cot = (inputs, wide_cut), (cotangent, wide_cut)
    rows_out, wide_out, chan_out = (sds(*ROWS), rows_cut), (sds(*WIDE), wide_cut), (sds(*CHAN), whole_cut)
    vchan = pltpu.VMEM(CHAN, F32)
    small = 2 * 3 * 32 * 32 * 8192
    product = 2 * 3 * 1024 * 256 * 256

    (within,) = staged(within_body, [rows_out], [x, inner], flops=small, name="within")
    within_spread = exchange_dp(within)

    (x_chunks,) = staged(x_rows_body, [], [x], spreads=1, index=index, name="x_rows")
    x_chunks = exchange_seq(x_chunks)
    pre, spectrum, unmixed, mixed_chunks = staged(
        forward_body, [chan_out] * 3, [first, twid, second, spectral, inverse_second, inverse_1st],
        [x_chunks], 1, 1, index, scratch=[vchan], flops=4 * product, name="forward",
    )
    mixed_chunks = exchange_seq(mixed_chunks)

    (gate_spread,) = staged(
        gate_body, [rows_out], [(within_spread, rows_cut), outer], after=[pre], flops=small,
        name="gate",
    )
    gate = exchange_dp(gate_spread)
    (weighed,) = staged(weigh_body, [rows_out], [cot], [mixed_chunks], index=index, name="weigh")
    across_grad, grad_chunks = staged(
        gate_grad_body, [rows_out], [(weighed, rows_cut), (gate, rows_cut), cot], spreads=1,
        index=index, name="gate_grad",
    )
    across_grad_spread = exchange_dp(across_grad)
    (output,) = staged(
        output_body, [wide_out], [x, (gate, rows_cut)], [mixed_chunks], index=index,
        after=[grad_chunks[0]], name="output",
    )
    grad_chunks = exchange_seq(grad_chunks)

    series, kernel_grad, keep, send = staged(
        backward_body,
        [(sds(*ROWS), whole_cut), (sds(4, 256, 256), whole_cut)] + [(sds(640, 256), whole_cut)] * 2,
        [
            inverse_1st, (unmixed, whole_cut), inverse_second, spectral, (spectrum, whole_cut), second,
            twid, (pre, whole_cut), first,
        ],
        [grad_chunks, x_chunks], 0, 1, index, [output],
        [vchan, vchan, vchan, vchan, pltpu.VMEM((1280, 256), F32)],
        flops=8 * product, name="backward",
    )
    (within_grad_spread,) = staged(
        within_grad_body, [rows_out], [(across_grad_spread, rows_cut), outer], after=[keep],
        flops=small, name="within_grad",
    )
    within_grad = exchange_dp(within_grad_spread)
    got = swap_core(send)
    quarters = small_call(
        sum_core_body, [(160, 256)] * XS, [keep, got], [pltpu.VMEM((640, 256), F32)],
        hold(index, [within_grad_spread]), name="sum_core",
    )
    (outer_part,) = staged(
        outer_grad_body, [(sds(32, 32), None)],
        [(across_grad_spread, rows_cut), (within_spread, rows_cut)], after=[quarters[0]],
        flops=small, limit=NEAR, name="outer_grad",
    )
    quarters = [quarters[0]] + [shift_x(quarters[k], k) for k in range(1, XS)]
    parts = small_call(
        sum_x_body, [(40, 256)] * YS, quarters, [pltpu.VMEM((160, 256), F32)], index, [outer_part],
        "sum_x",
    )
    parts = [parts[0]] + [shift_y(parts[k], k) for k in range(1, YS)]
    (part,) = small_call(sum_y_body, [(40, 256)], parts, name="sum_y")
    series = lax.all_to_all(hold(series, [part]), "seq", 0, 0, tiled=True)
    for flip in (1, 2, 4):
        (part,) = small_call(add_body, [(40, 256)], [part, swap_dp(part, flip)], name="sum_z")
    (gate_part,) = staged(
        inner_grad_body, [(sds(16, 256), None)],
        [(within_grad, rows_cut), x, (outer_part, whole_cut)], after=[part],
        scratch=[pltpu.VMEM((32, 32), F32)], flops=small, limit=NEAR, name="inner_grad",
    )
    parts = [part] + [shift_y(part, k) for k in range(1, YS)]
    (part,) = small_call(
        join_y_body, [(176, 256)], parts + [gate_part], index=index, name="join_y"
    )
    (input_grad,) = staged(
        input_grad_body, [wide_out],
        [cot, (series, rows_cut), (within_grad, rows_cut), inner], after=[part], flops=small,
        limit=NEAR, name="input_grad",
    )
    parts = [part] + [shift_x(part, k) for k in range(1, XS)]
    (half,) = small_call(
        join_x_body, [(656, 256)], parts, [pltpu.VMEM((XS, 16, 256), F32)],
        hold(index, [input_grad]), name="join_x",
    )
    *totals, inner_total, outer_total = small_call(
        join_core_body, [(256, 256)] * 5 + [(32, 32)] * 2, [half, swap_core(half)],
        [pltpu.VMEM((1280, 256), F32)], index, name="join_core",
    )
    first_total, second_total, inverse_second_total, inverse_first_total, twiddle_total = totals
    return (
        output,
        input_grad,
        first_total,
        second_total,
        inverse_second_total,
        inverse_first_total,
        twiddle_total,
        kernel_grad,
        inner_total[None],
        outer_total[None],
    )


def solution(mesh):
    wide = P("dp", "seq")
    gate = P("dp", None, None)
    spectral = P(("dp", "seq"), None, None)
    return jax.shard_map(
        per_device,
        mesh=mesh,
        in_specs=(wide, wide, P(), P(), P(), P(), P(), spectral, gate, gate),
        out_specs=(wide, wide, P(), P(), P(), P(), P(), spectral, gate, gate),
        check_vma=False,
    )
```

```python
import functools

import jax
import jax.numpy as jnp
from jax import lax
from jax.experimental import pallas as pl
from jax.experimental.pallas import tpu as pltpu
from jax.sharding import PartitionSpec as P

F32 = jnp.float32
BF16 = jnp.bfloat16
MIB = 1024 * 1024

NN = (((1,), (0,)), ((), ()))
NT = (((1,), (1,)), ((), ()))
TN = (((0,), (0,)), ((), ()))

SEQ = 8
XS = 4
YS = 4
ZS = 8


def sds(*shape):
    return jax.ShapeDtypeStruct(shape, F32)


VMEM = pl.BlockSpec(memory_space=pltpu.VMEM)
SMEM = pl.BlockSpec(memory_space=pltpu.SMEM)
HBM = pl.BlockSpec(memory_space=pltpu.HBM)
ANY = pl.BlockSpec(memory_space=pl.ANY)

ROWS = (32, 64, 128)
CHUNK = (4, 64, 128)
WIDE = (32, 8192)
CHAN = (1024, 256)
FULL = int(63.7 * MIB)
NEAR = int(62.9 * MIB)
PARTS = 4
PAIRS = 64 // PARTS // 2


def wide_cut(p):
    return (slice(None), pl.ds(p * 2048, 2048))


def rows_cut(p):
    return (slice(None), pl.ds(p * 16, 16)) if p < PARTS else None


def whole_cut(p):
    return (slice(None),) if p == 0 else None


class Flow:
    def __init__(self):
        self.coming, self.leaving, self.sent = {}, {}, []

    def need(self, k):
        for c in self.coming.pop(k, []):
            c.wait()

    def flush(self, k):
        for c in self.leaving.pop(k, []):
            c.start()
            self.sent.append(c)


def staged(
    body, outs, args, gathers=(), spreads=0, parts=PARTS, index=None, after=(), scratch=(),
    flops=0, limit=FULL, name=None,
):
    n_in, n_out, n_after = len(args), len(outs), len(after)
    flat = [c for g in gathers for c in g]
    chunk_outs = [sds(*CHUNK)] * (SEQ * spreads)
    cut_in = [k for k in range(n_in) if args[k][1] is not None]
    cut_out = [k for k in range(n_out) if outs[k][1] is not None]

    def kernel(*refs):
        refs = list(refs)

        def take(n):
            taken = refs[:n]
            del refs[:n]
            return taken

        place = take(1)[0] if index is not None else None
        in_refs, chunk_refs, _ = take(n_in), take(len(flat)), take(n_after)
        out_refs, spread_refs = take(n_out), take(len(chunk_outs))
        in_bufs, gathered = take(len(cut_in)), take(len(gathers))
        out_bufs, spread = take(len(cut_out)), take(spreads)
        sems = take(1)[0]
        count = [0]

        def copy(source, target):
            made = pltpu.make_async_copy(source, target, sems.at[count[0]])
            count[0] += 1
            return made

        flow = Flow()
        ins, results = list(in_refs), list(out_refs)

        def gather(g):
            arriving = []
            for i in range(SEQ):
                at = pl.ds(lax.rem(place[0] + SEQ - i, SEQ) * 4, 4)
                arriving.append(copy(chunk_refs[g * SEQ + i], gathered[g].at[at]))
                arriving[-1].start()
            flow.coming["rows", g] = arriving

        if gathers:
            gather(0)
        for b, k in enumerate(cut_in):
            ins[k] = in_bufs[b]
        for p in range(parts):
            for b, k in enumerate(cut_in):
                at = args[k][1](p)
                if at is not None:
                    made = copy(in_refs[k].at[at], in_bufs[b].at[at])
                    made.start()
                    flow.coming.setdefault(k if parts == 1 else (k, p), []).append(made)
        for g in range(1, len(gathers)):
            gather(g)
        for b, k in enumerate(cut_out):
            results[k] = out_bufs[b]
            for p in range(parts):
                at = outs[k][1](p)
                if at is not None:
                    flow.leaving.setdefault(k if parts == 1 else (k, p), []).append(
                        copy(out_bufs[b].at[at], out_refs[k].at[at])
                    )
        for s in range(spreads):
            for p in range(parts):
                at = pl.ds(p * (64 // parts), 64 // parts)
                flow.leaving["rows", s, p] = [
                    copy(
                        spread[s].at[pl.ds(lax.rem(place[0] + i, SEQ) * 4, 4), at],
                        spread_refs[s * SEQ + i].at[:, at],
                    )
                    for i in range(SEQ)
                ]
        for p in range(parts):
            if parts > 1:
                for g in range(len(gathers)):
                    flow.need(("rows", g))
                for k in cut_in:
                    flow.need((k, p))
            body(p, flow, ins, gathered, results, spread, refs + [place])
            if parts > 1:
                for k in cut_out:
                    flow.flush((k, p))
                for s in range(spreads):
                    flow.flush(("rows", s, p))
        for k in list(flow.coming):
            flow.need(k)
        for k in list(flow.leaving):
            flow.flush(k)
        for c in flow.sent:
            c.wait()

    operands = [a for a, _ in args] + flat + list(after)
    specs = [VMEM if cut is None else ANY for _, cut in args] + [ANY] * (len(flat) + n_after)
    if index is not None:
        operands, specs = [index] + operands, [SMEM] + specs
    n_sems = len(cut_in) * parts + len(flat) + (len(cut_out) + len(chunk_outs)) * parts
    moved = sum(4 * a.size for a, _ in args) + sum(4 * o.size for o, _ in outs)
    moved += sum(4 * c.size for c in flat) + sum(4 * c.size for c in chunk_outs)
    buffers = [pltpu.VMEM(args[k][0].shape, F32) for k in cut_in]
    buffers += [pltpu.VMEM(ROWS, F32)] * len(gathers)
    buffers += [pltpu.VMEM(outs[k][0].shape, F32) for k in cut_out]
    buffers += [pltpu.VMEM(ROWS, F32)] * spreads
    result = list(
        pl.pallas_call(
            kernel,
            out_shape=[o for o, _ in outs] + chunk_outs,
            in_specs=specs,
            out_specs=[VMEM if cut is None else ANY for _, cut in outs] + [ANY] * len(chunk_outs),
            scratch_shapes=buffers + [pltpu.SemaphoreType.DMA((max(n_sems, 1),))] + list(scratch),
            compiler_params=pltpu.CompilerParams(vmem_limit_bytes=limit),
            cost_estimate=pl.CostEstimate(flops=flops, bytes_accessed=moved, transcendentals=0),
            name=name,
        )(*operands)
    )
    return result[:n_out] + [result[n_out + SEQ * s : n_out + SEQ * (s + 1)] for s in range(spreads)]


def hold(array, after):
    def kernel(*refs):
        del refs

    return pl.pallas_call(
        kernel,
        out_shape=jax.ShapeDtypeStruct(array.shape, array.dtype),
        in_specs=[ANY] * (1 + len(after)),
        out_specs=ANY,
        input_output_aliases={0: 0},
        compiler_params=pltpu.CompilerParams(vmem_limit_bytes=NEAR),
        name="hold",
    )(array, *after)


def small_call(body, outs, args, scratch=(), index=None, after=(), name=None):
    operands, specs, lead = list(args), [VMEM] * len(args), len(args)
    if index is not None:
        operands, specs, lead = [index] + operands, [SMEM] + specs, lead + 1

    def kernel(*refs):
        body(*refs[:lead], *refs[lead + len(after) :])

    return list(
        pl.pallas_call(
            kernel,
            out_shape=[sds(*o) for o in outs],
            in_specs=specs + [ANY] * len(after),
            out_specs=[VMEM] * len(outs),
            scratch_shapes=list(scratch),
            compiler_params=pltpu.CompilerParams(vmem_limit_bytes=8 * MIB),
            name=name,
        )(*operands, *after)
    )


def split(value):
    high = value.astype(BF16)
    return high, (value - high.astype(F32)).astype(BF16)


def dot3(left, right, form):
    (lh, ll), (rh, rl) = left, right
    dot = functools.partial(lax.dot_general, dimension_numbers=form, preferred_element_type=F32)
    return dot(lh, rh) + (dot(lh, rl) + dot(ll, rh))


def stack(weight):
    return jnp.concatenate(weight, axis=0), weight[0]


def mix(weight, block):
    both, high = weight
    dot = functools.partial(lax.dot_general, dimension_numbers=NN, preferred_element_type=F32)
    product = dot(both, block[0])
    return product[:32] + (dot(high, block[1]) + product[32:])


def aligned(offset, step):
    return pl.multiple_of(offset, step)


def pairs_of(p):
    return range(p * PAIRS, (p + 1) * PAIRS)


def columns(j):
    return slice(j * 256, (j + 1) * 256)


def get_rows(ref, j):
    return jnp.concatenate([ref[:, 2 * j, :], ref[:, 2 * j + 1, :]], axis=1)


def put_rows(ref, j, value):
    ref[:, 2 * j, :] = value[:, :128]
    ref[:, 2 * j + 1, :] = value[:, 128:]


def within_body(p, flow, ins, gathered, outs, spread, scratch):
    x, inner = ins
    weight = stack(split(inner[...]))
    for j in pairs_of(p):
        put_rows(outs[0], j, mix(weight, split(x[:, columns(j)])))


def x_rows_body(p, flow, ins, gathered, outs, spread, scratch):
    for j in pairs_of(p):
        put_rows(spread[0], j, ins[0][:, columns(j)])


def gate_body(p, flow, ins, gathered, outs, spread, scratch):
    within, outer = ins
    weight = stack(split(outer[...]))
    for j in pairs_of(p):
        put_rows(outs[0], j, jax.nn.sigmoid(mix(weight, split(get_rows(within, j)))))


def weigh_body(p, flow, ins, gathered, outs, spread, scratch):
    for j in pairs_of(p):
        put_rows(outs[0], j, ins[0][:, columns(j)] * get_rows(gathered[0], j))


def gate_grad_body(p, flow, ins, gathered, outs, spread, scratch):
    weighed, gate, cot = ins
    at = (slice(None), slice(p * 16, (p + 1) * 16))
    g = gate[at]
    outs[0][at] = weighed[at] * g * (1.0 - g)
    for j in pairs_of(p):
        put_rows(spread[0], j, cot[:, columns(j)] * get_rows(gate, j))


def output_body(p, flow, ins, gathered, outs, spread, scratch):
    x, gate = ins
    for j in pairs_of(p):
        outs[0][:, columns(j)] = x[:, columns(j)] + get_rows(gathered[0], j) * get_rows(gate, j)


def within_grad_body(p, flow, ins, gathered, outs, spread, scratch):
    across_grad, outer = ins
    weight = stack(split(outer[...].T))
    for j in pairs_of(p):
        put_rows(outs[0], j, mix(weight, split(get_rows(across_grad, j))))


def outer_grad_body(p, flow, ins, gathered, outs, spread, scratch):
    total = outs[0][...] if p else jnp.zeros((32, 32), F32)
    for j in pairs_of(p):
        total = total + dot3(split(get_rows(ins[0], j)), split(get_rows(ins[1], j)), NT)
    outs[0][...] = total


def inner_grad_body(p, flow, ins, gathered, outs, spread, scratch):
    within_grad, x, outer_part = ins
    held = scratch[0]
    total = held[...] if p else jnp.zeros((32, 32), F32)
    for j in pairs_of(p):
        total = total + dot3(split(get_rows(within_grad, j)), split(x[:, columns(j)]), NT)
    held[...] = total
    if p == PARTS - 1:
        out = outs[0]
        out[...] = jnp.zeros_like(out)
        for k in range(2):
            rows = slice(16 * k, 16 * k + 16)
            out[:, 128 * k : 128 * k + 32] = held[rows, :]
            out[:, 128 * k + 32 : 128 * k + 64] = outer_part[rows, :]


def input_grad_body(p, flow, ins, gathered, outs, spread, scratch):
    cot, series, within_grad, inner = ins
    if p == 0:
        outs[1][...] = jnp.zeros((8, 128), F32)
    weight = stack(split(inner[...].T))
    for j in pairs_of(p):
        product = mix(weight, split(get_rows(within_grad, j)))
        outs[0][:, columns(j)] = (cot[:, columns(j)] + get_rows(series, j)) + product


def assemble(c, chunks, out, start):
    for s in range(SEQ):
        at = slice(start + s * 32, start + (s + 1) * 32)
        out[at, 0:128] = chunks[s * 4 + c, pl.ds(0, 32, stride=2), :]
        out[at, 128:256] = chunks[s * 4 + c, pl.ds(1, 32, stride=2), :]


def disperse(c, value, chunks):
    for s in range(SEQ):
        rows = value[s * 32 : (s + 1) * 32, :]
        chunks[s * 4 + c, pl.ds(0, 32, stride=2), :] = rows[:, :128]
        chunks[s * 4 + c, pl.ds(1, 32, stride=2), :] = rows[:, 128:]


def channel(c):
    return slice(c * 256, (c + 1) * 256)


def forward_body(p, flow, ins, gathered, outs, spread, scratch):
    first, twiddle, second, kernel, inverse_second, inverse_first = ins
    pre, spectrum, unmixed = outs
    x = scratch[0]
    flow.need(("rows", 0))
    flow.need(0)
    weight = split(first[...])
    for c in range(4):
        assemble(c, gathered[0], x, c * 256)
        pre[channel(c), :] = dot3(split(x[channel(c), :]), weight, NT)
    flow.flush(0)
    flow.need(1)
    flow.need(2)
    weight = split(second[...])
    for c in range(4):
        spectrum[channel(c), :] = dot3(weight, split(twiddle[...] * pre[channel(c), :]), NN)
    flow.flush(1)
    flow.need(3)
    flow.need(4)
    weight = split(inverse_second[...])
    for c in range(4):
        unmixed[channel(c), :] = dot3(weight, split(kernel[c].T * spectrum[channel(c), :]), NN)
    flow.flush(2)
    flow.need(5)
    weight = split(inverse_first[...])
    for c in range(4):
        disperse(c, dot3(split(unmixed[channel(c), :]), weight, NT), spread[0])


def add_up(terms):
    total = terms[0]
    for term in terms[1:]:
        total = total + term
    return total


def backward_body(p, flow, ins, gathered, outs, spread, scratch):
    inverse_first, unmixed, inverse_second, kernel, spectrum, second, twiddle, pre, first = ins
    series, kernel_grad, keep, send = outs
    x, mixed_grad, work, unmixed_grad, total, place = scratch
    flow.need(("rows", 0))
    flow.need(0)
    weight = split(inverse_first[...])
    for c in range(4):
        assemble(c, gathered[0], mixed_grad, c * 256)
        unmixed_grad[channel(c), :] = dot3(split(mixed_grad[channel(c), :]), weight, NN)
    flow.need(1)
    total[768:1024, :] = dot3(split(mixed_grad[...]), split(unmixed[...]), TN)
    flow.need(2)
    flow.need(3)
    flow.need(4)
    weight = split(inverse_second[...].T)
    terms = []
    for c in range(4):
        du = split(unmixed_grad[channel(c), :])
        kt = kernel[c].T
        sp = spectrum[channel(c), :]
        dsc = dot3(weight, du, NN)
        kernel_grad[c] = (dsc * sp).T
        work[channel(c), :] = dsc * kt
        terms.append(dot3(du, split(kt * sp), NT))
    total[512:768, :] = add_up(terms)
    flow.flush(1)
    flow.need(5)
    flow.need(6)
    flow.need(7)
    weight = split(second[...].T)
    terms, twiddles = [], []
    for c in range(4):
        dsp = split(work[channel(c), :])
        ds = dot3(weight, dsp, NN)
        product = pre[channel(c), :]
        terms.append(dot3(dsp, split(twiddle[...] * product), NT))
        twiddles.append(ds * product)
        mixed_grad[channel(c), :] = ds * twiddle[...]
    total[256:512, :] = add_up(terms)
    total[1024:1280, :] = add_up(twiddles)
    flow.need(("rows", 1))
    flow.need(8)
    weight = split(first[...])
    for c in range(4):
        assemble(c, gathered[1], x, c * 256)
        disperse(c, dot3(split(mixed_grad[channel(c), :]), weight, NN), series)
    flow.flush(0)
    total[0:256, :] = dot3(split(mixed_grad[...]), split(x[...]), TN)
    core = lax.rem(place[0], 2)
    keep[...] = total[pl.ds(aligned(core * 640, 640), 640), :]
    send[...] = total[pl.ds(aligned((1 - core) * 640, 640), 640), :]


def sum_core_body(index, keep, got, *refs):
    outs, total = refs[:XS], refs[XS]
    total[...] = keep[...] + got[...]
    place = index[0] // 2
    for k in range(XS):
        outs[k][...] = total[pl.ds(aligned(lax.rem(place + k, XS) * 160, 160), 160), :]


def sum_x_body(index, a, b, c, d, *refs):
    outs, total = refs[:YS], refs[YS]
    total[...] = (a[...] + b[...]) + (c[...] + d[...])
    place = index[1] // ZS
    for k in range(YS):
        outs[k][...] = total[pl.ds(aligned(lax.rem(place + k, YS) * 40, 40), 40), :]


def sum_y_body(a, b, c, d, out):
    out[...] = (a[...] + b[...]) + (c[...] + d[...])


def add_body(a, b, out):
    out[...] = a[...] + b[...]


def join_y_body(index, a, b, c, d, gate_part, out):
    place = index[1] // ZS
    for k, part in enumerate((a, b, c, d)):
        origin = lax.rem(place + YS - k, YS)
        out[pl.ds(aligned(origin * 40, 40), 40), :] = part[...]
    out[160:176, :] = gate_part[...]


def join_x_body(index, a, b, c, d, out, slots):
    place = index[0] // 2
    for k, part in enumerate((a, b, c, d)):
        origin = lax.rem(place + XS - k, XS)
        out[pl.ds(aligned(origin * 160, 160), 160), :] = part[0:160, :]
        slots[origin] = part[160:176, :]
    out[640:656, :] = (slots[0] + slots[1]) + (slots[2] + slots[3])


def join_core_body(index, mine, other, *refs):
    outs, (inner, outer, total) = refs[:5], refs[5:]
    core = lax.rem(index[0], 2)
    total[pl.ds(aligned(core * 640, 640), 640), :] = mine[0:640, :]
    total[pl.ds(aligned((1 - core) * 640, 640), 640), :] = other[0:640, :]
    for k in range(5):
        outs[k][...] = total[k * 256 : (k + 1) * 256, :]
    gate = mine[640:656, :] + other[640:656, :]
    for k in range(2):
        rows = slice(16 * k, 16 * k + 16)
        inner[rows, :] = gate[:, 128 * k : 128 * k + 32]
        outer[rows, :] = gate[:, 128 * k + 32 : 128 * k + 64]


def exchange_seq(chunks):
    return [chunks[0]] + [
        lax.ppermute(chunks[i], "seq", [(s, (s + i) % SEQ) for s in range(SEQ)])
        for i in range(1, SEQ)
    ]


def swap_core(value):
    return lax.ppermute(value, "seq", [(s, s ^ 1) for s in range(SEQ)])


def shift_x(value, k):
    return lax.ppermute(value, "seq", [(s, (s + 2 * k) % SEQ) for s in range(SEQ)])


def shift_y(value, k):
    pairs = [(y * ZS + z, (y + k) % YS * ZS + z) for y in range(YS) for z in range(ZS)]
    return lax.ppermute(value, "dp", pairs)


def swap_dp(value, flip):
    return lax.ppermute(value, "dp", [(d, d ^ flip) for d in range(YS * ZS)])


def exchange_dp(value):
    return lax.all_to_all(value, "dp", 0, 0, tiled=True)


def per_device(
    inputs,
    cotangent,
    first_factor,
    second_sequence_factor,
    inverse_second_factor,
    inverse_first,
    twiddle,
    kernel,
    gate_inner,
    gate_outer,
):
    index = jnp.stack([lax.axis_index("seq"), lax.axis_index("dp")]).astype(jnp.int32)
    inner, outer = (gate_inner[0], whole_cut), (gate_outer[0], whole_cut)
    first, second, inverse_second, inverse_1st, twid, spectral = [
        (f, whole_cut)
        for f in (
            first_factor, second_sequence_factor, inverse_second_factor, inverse_first, twiddle, kernel
        )
    ]
    x, cot = (inputs, wide_cut), (cotangent, wide_cut)
    rows_out, wide_out, chan_out = (sds(*ROWS), rows_cut), (sds(*WIDE), wide_cut), (sds(*CHAN), whole_cut)
    vchan = pltpu.VMEM(CHAN, F32)
    small = 2 * 3 * 32 * 32 * 8192
    product = 2 * 3 * 1024 * 256 * 256

    (within,) = staged(within_body, [rows_out], [x, inner], flops=small, name="within")
    within_spread = exchange_dp(within)

    (x_chunks,) = staged(x_rows_body, [], [x], spreads=1, index=index, name="x_rows")
    x_chunks = exchange_seq(x_chunks)
    pre, spectrum, unmixed, mixed_chunks = staged(
        forward_body, [chan_out] * 3, [first, twid, second, spectral, inverse_second, inverse_1st],
        [x_chunks], 1, 1, index, scratch=[vchan], flops=4 * product, name="forward",
    )
    mixed_chunks = exchange_seq(mixed_chunks)

    (gate_spread,) = staged(
        gate_body, [rows_out], [(within_spread, rows_cut), outer], after=[pre], flops=small,
        name="gate",
    )
    gate = exchange_dp(gate_spread)
    (weighed,) = staged(weigh_body, [rows_out], [cot], [mixed_chunks], index=index, name="weigh")
    across_grad, grad_chunks = staged(
        gate_grad_body, [rows_out], [(weighed, rows_cut), (gate, rows_cut), cot], spreads=1,
        index=index, name="gate_grad",
    )
    across_grad_spread = exchange_dp(across_grad)
    (output,) = staged(
        output_body, [wide_out], [x, (gate, rows_cut)], [mixed_chunks], index=index,
        after=[grad_chunks[0]], name="output",
    )
    grad_chunks = exchange_seq(grad_chunks)

    series, kernel_grad, keep, send = staged(
        backward_body,
        [(sds(*ROWS), whole_cut), (sds(4, 256, 256), whole_cut)] + [(sds(640, 256), whole_cut)] * 2,
        [
            inverse_1st, (unmixed, whole_cut), inverse_second, spectral, (spectrum, whole_cut), second,
            twid, (pre, whole_cut), first,
        ],
        [grad_chunks, x_chunks], 0, 1, index, [output],
        [vchan, vchan, vchan, vchan, pltpu.VMEM((1280, 256), F32)],
        flops=8 * product, name="backward",
    )
    (within_grad_spread,) = staged(
        within_grad_body, [rows_out], [(across_grad_spread, rows_cut), outer], after=[keep],
        flops=small, name="within_grad",
    )
    within_grad = exchange_dp(within_grad_spread)
    got = swap_core(send)
    quarters = small_call(
        sum_core_body, [(160, 256)] * XS, [keep, got], [pltpu.VMEM((640, 256), F32)],
        hold(index, [within_grad_spread]), name="sum_core",
    )
    (outer_part,) = staged(
        outer_grad_body, [(sds(32, 32), None)],
        [(across_grad_spread, rows_cut), (within_spread, rows_cut)], after=[quarters[0]],
        flops=small, limit=NEAR, name="outer_grad",
    )
    quarters = [quarters[0]] + [shift_x(quarters[k], k) for k in range(1, XS)]
    parts = small_call(
        sum_x_body, [(40, 256)] * YS, quarters, [pltpu.VMEM((160, 256), F32)], index, [outer_part],
        "sum_x",
    )
    parts = [parts[0]] + [shift_y(parts[k], k) for k in range(1, YS)]
    (part,) = small_call(sum_y_body, [(40, 256)], parts, name="sum_y")
    series = lax.all_to_all(hold(series, [part]), "seq", 0, 0, tiled=True)
    for flip in (1, 2, 4):
        (part,) = small_call(add_body, [(40, 256)], [part, swap_dp(part, flip)], name="sum_z")
    (gate_part,) = staged(
        inner_grad_body, [(sds(16, 256), None)],
        [(within_grad, rows_cut), x, (outer_part, whole_cut)], after=[part],
        scratch=[pltpu.VMEM((32, 32), F32)], flops=small, limit=NEAR, name="inner_grad",
    )
    parts = [part] + [shift_y(part, k) for k in range(1, YS)]
    (part,) = small_call(
        join_y_body, [(176, 256)], parts + [gate_part], index=index, name="join_y"
    )
    input_grad, input_grad_done = staged(
        input_grad_body, [wide_out, (sds(8, 128), whole_cut)],
        [cot, (series, rows_cut), (within_grad, rows_cut), inner], after=[part], flops=small,
        limit=NEAR, name="input_grad",
    )
    parts = [part] + [shift_x(part, k) for k in range(1, XS)]
    (half,) = small_call(
        join_x_body, [(656, 256)], parts, [pltpu.VMEM((XS, 16, 256), F32)], index,
        [input_grad_done], "join_x",
    )
    *totals, inner_total, outer_total = small_call(
        join_core_body, [(256, 256)] * 5 + [(32, 32)] * 2, [half, swap_core(half)],
        [pltpu.VMEM((1280, 256), F32)], index, name="join_core",
    )
    first_total, second_total, inverse_second_total, inverse_first_total, twiddle_total = totals
    return (
        output,
        input_grad,
        first_total,
        second_total,
        inverse_second_total,
        inverse_first_total,
        twiddle_total,
        kernel_grad,
        inner_total[None],
        outer_total[None],
    )


def solution(mesh):
    wide = P("dp", "seq")
    gate = P("dp", None, None)
    spectral = P(("dp", "seq"), None, None)
    return jax.shard_map(
        per_device,
        mesh=mesh,
        in_specs=(wide, wide, P(), P(), P(), P(), P(), spectral, gate, gate),
        out_specs=(wide, wide, P(), P(), P(), P(), P(), spectral, gate, gate),
        check_vma=False,
    )
```
